128 devices in a mesh: lat: 8 (over z_hi, x), lon: 16 (over z_lo, y, core).
Axes of the slice: x: 4, y: 4, z: 4 (z_hi: 2, z_lo: 2; z = z_hi * 2 + z_lo), core: 2. Of those that a mesh axis runs over, the one named last changes fastest.
Arguments:
- tokens: bfloat16 [512, 256, 512], P('lat', 'lon'), may hold values from -8 to 8
- region: int32 [512, 256], P('lat', 'lon'), may hold values from 0 to 2
- qkv_one: bfloat16 [512, 1536], replicated, may hold values from -6 to 6
- proj_one: bfloat16 [512, 512], replicated, may hold values from -0.25 to 0.25
- merge_weight: bfloat16 [2048, 1024], replicated, may hold values from -0.125 to 0.125
- qkv_two: bfloat16 [1024, 3072], replicated, may hold values from -6 to 6
- proj_two: bfloat16 [1024, 1024], replicated, may hold values from -0.1875 to 0.1875
- unmerge_weight: bfloat16 [1024, 2048], replicated, may hold values from -0.1875 to 0.1875
- cotangent: bfloat16 [512, 256, 512], P('lat', 'lon'), may hold values from -6 to 6
Outputs:
- output: bfloat16 [512, 256, 512], P('lat', 'lon')
- grad_tokens: bfloat16 [512, 256, 512], P('lat', 'lon')
- grad_qkv_two: float32 [1024, 3072], P(('lat', 'lon'))
- grad_proj_two: float32 [1024, 1024], P(('lat', 'lon'))
The draws below stay inside these ranges and needn't reach their ends.
Inputs may be any that keep to these rules, and one draw needn't show every extreme that they name: `region`: labels compared within a window of the shifted grid.
All inputs are finite; a program needn't handle non-finite values.
Results may differ from the reference program's by a relative error of at most 0.028.
Values may be sent and summed in bfloat16 or wider, within the bound.
A program may use at most 192 MiB of HBM per device.

```python
import math
import jax
import jax.numpy as jnp
from jax import lax

C1 = 512
C2 = 1024
HEAD = 64
WIN = 8
NLAT = 512
NLON = 256


def projection_weight(key, width, loud_share):
    drawn_key, pick_key, gain_key, forced_key = jax.random.split(key, 4)
    drawn_weight = jax.random.truncated_normal(drawn_key, -4.0, 4.0, (width, 3 * width), jnp.float32) * width ** (-0.5)
    head_count = width // HEAD
    chosen = jax.random.uniform(pick_key, (head_count,), jnp.float32) < loud_share
    forced = jax.random.randint(forced_key, (), 0, head_count)
    chosen = jnp.logical_or(chosen, jnp.logical_and(jnp.arange(head_count) == forced, loud_share > 0.0))
    loud_gain = jnp.sqrt(jnp.exp(jax.random.uniform(gain_key, (head_count,), jnp.float32, math.log(19.0), math.log(60.0))))
    factor = jnp.repeat(jnp.where(chosen, loud_gain, 1.0), HEAD)
    loud_cols = jnp.repeat(chosen, HEAD)
    query_cols = drawn_weight[:, :width] * factor
    aligned_cols = factor * (0.7 * drawn_weight[:, :width] + 0.714 * drawn_weight[:, width:2 * width])
    key_cols = jnp.where(loud_cols, aligned_cols, drawn_weight[:, width:2 * width])
    value_cols = drawn_weight[:, 2 * width:] / (factor * factor)
    return jnp.concatenate([query_cols, key_cols, value_cols], axis=1)


def draw_tokens(key, part):
    key = jax.random.fold_in(key, 11)
    noise_key = jax.random.fold_in(key, 0)
    noise_bound = 6.0
    noise_field = jax.random.truncated_normal(noise_key, -noise_bound, noise_bound, (NLAT, NLON, C1), jnp.float32)
    return noise_field.astype(jnp.bfloat16)


def draw_qkv_one(key, part):
    key = jax.random.fold_in(key, 23)
    loud_share = 0.0
    return projection_weight(key, C1, loud_share).astype(jnp.bfloat16)


def draw_qkv_two(key, part):
    key = jax.random.fold_in(key, 37)
    loud_share = 0.0
    return projection_weight(key, C2, loud_share).astype(jnp.bfloat16)


def place_ends(entries, rng, smallest, high):
    longest = entries.shape.index(max(entries.shape))
    spots = []
    for shift in (0, 1):
        where = [jax.random.randint(jax.random.fold_in(rng, axis), (), 0, length) for axis, length in enumerate(entries.shape)]
        where[longest] = (where[longest] + shift) % entries.shape[longest]
        spots.append(tuple(where))
    return entries.at[spots[0]].set(smallest).at[spots[1]].set(high)


def block_scale(stream_key, dims, cuts, smallest, largest):
    def one(axis_at, blocks):
        draws = jax.random.uniform(jax.random.fold_in(jax.random.fold_in(stream_key, 6), axis_at), (blocks,), jnp.float32, smallest / len(cuts), largest / len(cuts))
        return jnp.repeat(jnp.exp(draws), dims[axis_at] // blocks).reshape((-1,) + (1,) * (len(dims) - axis_at - 1))

    loudness = one(*cuts[0])
    for cut in cuts[1:]:
        loudness = loudness * one(*cut)
    return loudness


def gaussian(own_key, dims, scale, bound, pieces=(), dtype=jnp.bfloat16):
    entries = scale * jax.random.normal(own_key, dims, jnp.float32)
    if pieces:
        entries = entries * block_scale(own_key, dims, pieces, -0.22, 0.18)
    return jnp.clip(entries, -bound, bound).astype(dtype)


def setup_inputs(seed: int = 0) -> dict:
    keys = jax.random.split(jax.random.key(seed), 10)
    tokens = draw_tokens(jax.random.fold_in(keys[9], 71), 0)
    region = place_ends(jax.random.randint(keys[1], (NLAT, NLON), 0, 3), jax.random.fold_in(keys[1], 1), 0, 2).astype(jnp.int32)
    qkv_one = draw_qkv_one(jax.random.fold_in(keys[9], 71), 0)
    proj_one = gaussian(keys[3], (C1, C1), C1 ** -0.5, 0.25)
    merge_weight = gaussian(keys[4], (4 * C1, C2), (4 * C1) ** -0.5, 0.125)
    qkv_two = draw_qkv_two(jax.random.fold_in(keys[9], 71), 0)
    proj_two = gaussian(keys[6], (C2, C2), C2 ** -0.5, 0.1875)
    unmerge_weight = gaussian(keys[7], (C2, 4 * C1), C2 ** -0.5, 0.1875)
    cotangent = gaussian(keys[8], (NLAT, NLON, C1), 1.0, 6.0, ((0, 8), (1, 16)))
    return {"tokens": tokens, "region": region, "qkv_one": qkv_one, "proj_one": proj_one, "merge_weight": merge_weight, "qkv_two": qkv_two, "proj_two": proj_two, "unmerge_weight": unmerge_weight, "cotangent": cotangent}


def layer_norm(field):
    values = field.astype(jnp.float32)
    centered = values - lax.optimization_barrier(jnp.mean(values, axis=-1, keepdims=True))
    spread = lax.optimization_barrier(jnp.mean(centered * centered, axis=-1, keepdims=True))
    return centered * lax.rsqrt(spread + 1e-05)

def attend(queries, key_rows, value_rows, allowed):
    batch, length, width = queries.shape
    split_shape = (batch, length, width // HEAD, HEAD)
    scores = jnp.einsum('bqhd,bkhd->bhqk', queries.reshape(split_shape).astype(jnp.float32), key_rows.reshape(split_shape).astype(jnp.float32)) * HEAD ** (-0.5)
    if allowed is not None:
        scores = jnp.where(allowed[:, None], scores, -1e+30)
    highest = lax.optimization_barrier(jnp.max(scores, axis=-1, keepdims=True))
    expo = jnp.exp(scores - highest)
    softmax_weights = (expo / lax.optimization_barrier(jnp.sum(expo, axis=-1, keepdims=True))).astype(jnp.bfloat16)
    mixed = jnp.einsum('bhqk,bkhd->bqhd', softmax_weights.astype(jnp.float32), value_rows.reshape(split_shape).astype(jnp.float32))
    return mixed.astype(jnp.bfloat16).reshape(batch, length, width)

def to_windows(field):
    row_count, col_count = (field.shape[0], field.shape[1])
    trailing = field.shape[2:]
    grouped = field.reshape((row_count // WIN, WIN, col_count // WIN, WIN) + trailing)
    grouped = jnp.moveaxis(grouped, 2, 1)
    return grouped.reshape((row_count // WIN * (col_count // WIN), WIN * WIN) + trailing)

def from_windows(field, row_count, col_count):
    trailing = field.shape[2:]
    grouped = field.reshape((row_count // WIN, col_count // WIN, WIN, WIN) + trailing)
    grouped = jnp.moveaxis(grouped, 2, 1)
    return grouped.reshape((row_count, col_count) + trailing)

def level_one(shifted, region, qkv_one, proj_one):
    row_count, col_count, width = shifted.shape
    normed = layer_norm(shifted).astype(jnp.bfloat16)
    packed = jnp.dot(normed, qkv_one, preferred_element_type=jnp.float32).astype(jnp.bfloat16)
    windows = to_windows(packed)
    labels = to_windows(region)
    allowed = labels[:, :, None] == labels[:, None, :]
    mixed = attend(windows[..., :width], windows[..., width:2 * width], windows[..., 2 * width:], allowed)
    mixed = from_windows(mixed, row_count, col_count)
    return (shifted.astype(jnp.float32) + jnp.dot(mixed, proj_one, preferred_element_type=jnp.float32)).astype(jnp.bfloat16)

def merge_level(fine, merge_weight):
    row_count, col_count, width = fine.shape
    grouped = fine.reshape(row_count // 2, 2, col_count // 2, 2, width)
    grouped = jnp.moveaxis(grouped, 2, 1).reshape(row_count // 2, col_count // 2, 4 * width)
    return jnp.dot(layer_norm(grouped).astype(jnp.bfloat16), merge_weight, preferred_element_type=jnp.float32).astype(jnp.bfloat16)

def skip_up(coarse, unmerge_weight):
    row_count, col_count, _ = coarse.shape
    spread = jnp.dot(layer_norm(coarse).astype(jnp.bfloat16), unmerge_weight, preferred_element_type=jnp.float32)
    width = spread.shape[-1] // 4
    spread = jnp.moveaxis(spread.reshape(row_count, col_count, 2, 2, width), 2, 1)
    return spread.reshape(2 * row_count, 2 * col_count, width)

def row_attention(packed):
    width = packed.shape[-1] // 3
    return attend(packed[..., :width], packed[..., width:2 * width], packed[..., 2 * width:], None)

def norm_rounded(field):
    return layer_norm(field).astype(jnp.bfloat16)

def reference(tokens, region, qkv_one, proj_one, merge_weight, qkv_two, proj_two, unmerge_weight, cotangent):
    offset_cells = WIN // 2
    shifted = jnp.roll(tokens, (offset_cells, offset_cells), axis=(0, 1))
    y_shift, back_one = jax.vjp(lambda field: level_one(field, region, qkv_one, proj_one), shifted)
    fine = jnp.roll(y_shift, (-offset_cells, -offset_cells), axis=(0, 1))
    coarse, back_merge = jax.vjp(lambda field: merge_level(field, merge_weight), fine)
    width_two = coarse.shape[-1]
    normed_two = norm_rounded(coarse)
    packed_two = jnp.dot(normed_two, qkv_two, preferred_element_type=jnp.float32).astype(jnp.bfloat16)
    mixed_two, back_attend = jax.vjp(row_attention, packed_two)
    level_two = (coarse.astype(jnp.float32) + jnp.dot(mixed_two, proj_two, preferred_element_type=jnp.float32)).astype(jnp.bfloat16)
    upper, back_skip = jax.vjp(lambda field: skip_up(field, unmerge_weight), level_two)
    output = (fine.astype(jnp.float32) + upper).astype(jnp.bfloat16)
    grad_level, = back_skip(cotangent.astype(jnp.float32))
    flat_mixed = mixed_two.reshape(-1, width_two)
    grad_proj_two = jnp.dot(flat_mixed.T, grad_level.reshape(-1, width_two), preferred_element_type=jnp.float32)
    grad_mixed = jnp.dot(grad_level, proj_two.T, preferred_element_type=jnp.float32).astype(jnp.bfloat16)
    grad_packed, = back_attend(grad_mixed)
    grad_qkv_two = jnp.dot(normed_two.reshape(-1, width_two).T, grad_packed.reshape(-1, 3 * width_two), preferred_element_type=jnp.float32)
    grad_normed = jnp.dot(grad_packed, qkv_two.T, preferred_element_type=jnp.float32).astype(jnp.bfloat16)
    grad_norm_in, = jax.vjp(norm_rounded, coarse)[1](grad_normed)
    grad_coarse = (grad_level.astype(jnp.float32) + grad_norm_in.astype(jnp.float32)).astype(jnp.bfloat16)
    grad_merge_in, = back_merge(grad_coarse)
    grad_fine = (cotangent.astype(jnp.float32) + grad_merge_in.astype(jnp.float32)).astype(jnp.bfloat16)
    grad_shift = jnp.roll(grad_fine, (offset_cells, offset_cells), axis=(0, 1))
    grad_shifted, = back_one(grad_shift)
    grad_tokens = jnp.roll(grad_shifted, (-offset_cells, -offset_cells), axis=(0, 1))
    return (output, grad_tokens, grad_qkv_two, grad_proj_two)
```

```python
import itertools

import jax
import jax.numpy as jnp
from jax import lax
from jax.experimental import pallas as pl
from jax.experimental.pallas import tpu as pltpu
from jax.sharding import PartitionSpec as P

HEAD = 64
WIN = 8


def shifted_2(x, axis, by):
    devices = lax.axis_size(axis)
    return lax.ppermute(x, axis, [(i, (i + by) % devices) for i in range(devices)])


def layer_norm(field):
    values = field.astype(jnp.float32)
    centered = values - jnp.mean(values, axis=-1, keepdims=True)
    spread = jnp.mean(centered * centered, axis=-1, keepdims=True)
    return centered * lax.rsqrt(spread + 1e-05)


def attend(queries, key_rows, value_rows, allowed):
    batch, length, width = queries.shape
    split_shape = (batch, length, width // HEAD, HEAD)
    scores = jnp.einsum(
        "bqhd,bkhd->bhqk",
        queries.reshape(split_shape),
        key_rows.reshape(split_shape),
        preferred_element_type=jnp.float32,
    ) * HEAD ** (-0.5)
    if allowed is not None:
        scores = jnp.where(allowed[:, None], scores, -1e30)
    highest = jnp.max(scores, axis=-1, keepdims=True)
    expo = jnp.exp(scores - highest)
    softmax_weights = (expo / jnp.sum(expo, axis=-1, keepdims=True)).astype(jnp.bfloat16)
    mixed = jnp.einsum(
        "bhqk,bkhd->bqhd",
        softmax_weights,
        value_rows.reshape(split_shape),
        preferred_element_type=jnp.float32,
    )
    return mixed.astype(jnp.bfloat16).reshape(batch, length, width)


def to_windows(field):
    row_count, col_count = (field.shape[0], field.shape[1])
    trailing = field.shape[2:]
    grouped = field.reshape((row_count // WIN, WIN, col_count // WIN, WIN) + trailing)
    grouped = jnp.moveaxis(grouped, 2, 1)
    return grouped.reshape((row_count // WIN * (col_count // WIN), WIN * WIN) + trailing)


def from_windows(field, row_count, col_count):
    trailing = field.shape[2:]
    grouped = field.reshape((row_count // WIN, col_count // WIN, WIN, WIN) + trailing)
    grouped = jnp.moveaxis(grouped, 2, 1)
    return grouped.reshape((row_count, col_count) + trailing)


def level_one(shifted, region, qkv_one, proj_one):
    row_count, col_count, width = shifted.shape
    normed = layer_norm(shifted).astype(jnp.bfloat16)
    packed = jnp.dot(normed, qkv_one, preferred_element_type=jnp.float32).astype(jnp.bfloat16)
    windows = to_windows(packed)
    labels = to_windows(region)
    allowed = labels[:, :, None] == labels[:, None, :]
    mixed = attend(
        windows[..., :width], windows[..., width : 2 * width], windows[..., 2 * width :], allowed
    )
    mixed = from_windows(mixed, row_count, col_count)
    return (
        shifted.astype(jnp.float32) + jnp.dot(mixed, proj_one, preferred_element_type=jnp.float32)
    ).astype(jnp.bfloat16)


def merge_level(fine, merge_weight):
    row_count, col_count, width = fine.shape
    grouped = fine.reshape(row_count // 2, 2, col_count // 2, 2, width)
    grouped = jnp.moveaxis(grouped, 2, 1).reshape(row_count // 2, col_count // 2, 4 * width)
    return jnp.dot(
        layer_norm(grouped).astype(jnp.bfloat16), merge_weight, preferred_element_type=jnp.float32
    ).astype(jnp.bfloat16)


def skip_up(coarse, unmerge_weight):
    row_count, col_count, _ = coarse.shape
    spread = jnp.dot(
        layer_norm(coarse).astype(jnp.bfloat16), unmerge_weight, preferred_element_type=jnp.float32
    )
    width = spread.shape[-1] // 4
    spread = jnp.moveaxis(spread.reshape(row_count, col_count, 2, 2, width), 2, 1)
    return spread.reshape(2 * row_count, 2 * col_count, width)


def row_attention(packed):
    width = packed.shape[-1] // 3
    return attend(
        packed[..., :width], packed[..., width : 2 * width], packed[..., 2 * width :], None
    )


def norm_rounded(field):
    return layer_norm(field).astype(jnp.bfloat16)


def roll_forward(field):
    offset_cells = WIN // 2
    arrived = shifted_2(field[-offset_cells:], "lat", 1)
    field = jnp.concatenate([arrived, field[:-offset_cells]], axis=0)
    arrived = shifted_2(field[:, -offset_cells:], "lon", 1)
    return jnp.concatenate([arrived, field[:, :-offset_cells]], axis=1)


def roll_backward(field):
    offset_cells = WIN // 2
    arrived = shifted_2(field[:offset_cells], "lat", -1)
    field = jnp.concatenate([field[offset_cells:], arrived], axis=0)
    arrived = shifted_2(field[:, :offset_cells], "lon", -1)
    return jnp.concatenate([field[:, offset_cells:], arrived], axis=1)


def gather_rows(field):
    return lax.all_to_all(field, "lon", split_axis=0, concat_axis=1, tiled=True)


def return_rows(field):
    return lax.all_to_all(field, "lon", split_axis=1, concat_axis=0, tiled=True)


MESH = pl.DeviceIdType.MESH
BF = jnp.bfloat16
F32 = jnp.float32
VMEM_LIMIT = 60 * 1024 * 1024

FOLD = 2048
PARTS = ((0, 640, ("x", "y", "z")), (640, 1408, ("y", "z", "x")), (1408, 2048, ("z", "x", "y")))
LABELS = ("zh", "x", "zl", "y")


def coordinates():
    lat, lon = lax.axis_index("lat"), lax.axis_index("lon")
    return {
        "zh": lat // 4,
        "x": lat % 4,
        "zl": lon // 8,
        "y": (lon // 2) % 4,
        "core": lon % 2,
    }


def device_of(c):
    return (c["zh"] * 4 + c["x"], (c["zl"] * 4 + c["y"]) * 2 + c["core"])


def moved(c, axis, by):
    c = dict(c)
    if axis == "z":
        z = (c["zh"] * 2 + c["zl"] + by) % 4
        c["zh"], c["zl"] = z // 2, z % 2
    elif axis == "core":
        c["core"] = 1 - c["core"]
    else:
        c[axis] = (c[axis] + by) % 4
    return c


def pick(labels, axis, c):
    names = ("zh", "zl") if axis == "z" else (axis,)
    return tuple(c[label] if label in names else slice(None) for label in labels)


def drop(labels, axis):
    names = ("zh", "zl") if axis == "z" else (axis,)
    return tuple(label for label in labels if label not in names)


def sizes(labels):
    return tuple(4 if label in ("x", "y") else 2 for label in labels)


def reduce_scratch():
    shapes = [pltpu.VMEM((2, 4, 2, 4, 16, FOLD), BF)]
    for start, stop, order in PARTS:
        labels = LABELS
        for step, axis in enumerate(order):
            labels = drop(labels, axis)
            dtype = BF
            shapes.append(pltpu.VMEM((3,) + sizes(labels) + (16, stop - start), dtype))
            if step < 2:
                shapes.append(pltpu.VMEM(sizes(labels) + (16, stop - start), dtype))
    return shapes + [pltpu.SemaphoreType.DMA((3, 3, 3)), pltpu.SemaphoreType.DMA((3, 3, 3))]


class Reducer:
    def __init__(self, scratch):
        self.total = scratch[0]
        self.slots = [scratch[1 + 5 * p : 6 + 5 * p] for p in range(3)]
        self.send_sem, self.recv_sem = scratch[16], scratch[17]
        self.c = coordinates()

    def partners(self):
        return [moved(self.c, "core", 1)] + [
            moved(self.c, axis, by) for axis in ("x", "y", "z") for by in (1, 2, 3)
        ]

    def source(self, part, step):
        start, stop, order = PARTS[part]
        labels = LABELS
        for axis in order[:step]:
            labels = drop(labels, axis)
        if step == 0:
            return labels, self.total, (slice(None), pl.ds(start, stop - start))
        return labels, self.slots[part][2 * step - 1], (slice(None), slice(None))

    def copies(self, part, step):
        axis = PARTS[part][2][step]
        labels, source, rest = self.source(part, step)
        found = []
        for by in (2, 1, 3):
            target = moved(self.c, axis, by)
            found.append(
                pltpu.make_async_remote_copy(
                    src_ref=source.at[pick(labels, axis, target) + rest],
                    dst_ref=self.slots[part][2 * step].at[by - 1],
                    send_sem=self.send_sem.at[part, step, by - 1],
                    recv_sem=self.recv_sem.at[part, step, by - 1],
                    device_id=device_of(target),
                    device_id_type=MESH,
                )
            )
        return found

    def start(self, part, step):
        for copy in self.copies(part, step):
            copy.start()

    def finish(self, part, step):
        for copy in self.copies(part, step):
            copy.wait_recv()
        axis = PARTS[part][2][step]
        labels, source, rest = self.source(part, step)
        arrived = self.slots[part][2 * step]
        left = drop(labels, axis)
        for place in itertools.product(*[range(size) for size in sizes(left)]):
            where = dict(zip(left, place))
            where.update({k: self.c[k] for k in labels if k not in where})
            own = source[tuple(where[label] for label in labels) + rest].astype(F32)
            summed = own
            for slot in range(3):
                summed = summed + arrived[(slot,) + place].astype(F32)
            if step == 2:
                return summed
            self.slots[part][2 * step + 1][place] = summed.astype(BF)

    def drain(self):
        for part in range(3):
            for step in range(3):
                for copy in self.copies(part, step):
                    copy.wait_send()


def store_folded(part, summed, qkv_ref, proj_ref):
    start, stop, _ = PARTS[part]
    top, low = summed[:8], summed[8:]
    qkv_ref[:, start:stop] = top
    cut = min(max(1024 - start, 0), stop - start)
    if cut:
        qkv_ref[:, FOLD + start : FOLD + start + cut] = low[:, :cut]
    if cut < stop - start:
        proj_ref[:, start + cut - 1024 : stop - 1024] = low[:, cut:]


def operand_scratch():
    return [
        pltpu.VMEM((2, 512, 256), BF),
        pltpu.VMEM((2, 512, 256), BF),
        pltpu.VMEM((2, 512, 256), BF),
        pltpu.VMEM((2, 256, 3072), BF),
        pltpu.VMEM((2, 256, 1024), BF),
        pltpu.VMEM((64, 2, 8, 256), F32),
        pltpu.SemaphoreType.DMA((4,)),
        pltpu.SemaphoreType.DMA((4,)),
    ]


def weight_kernel(normed_ref, grad_ref, mixed_ref, level_ref, qkv_ref, proj_ref, *scratch):
    left_q, left_p, leave, right_q, right_p, turned, pair_send, pair_recv = scratch[:8]
    reducer = Reducer(scratch[8:])
    c = reducer.c
    other = device_of(moved(c, "core", 1))
    barrier = pltpu.get_barrier_semaphore()
    partners = reducer.partners()
    for partner in partners:
        pl.semaphore_signal(barrier, inc=1, device_id=device_of(partner), device_id_type=MESH)
    right_q[0] = grad_ref[...]
    right_p[0] = level_ref[...]
    turned[...] = normed_ref[...].astype(F32).T.reshape(64, 2, 8, 256)
    left_q[0] = turned[:, c["core"]].reshape(512, 256).astype(BF)
    leave[0] = turned[:, 1 - c["core"]].reshape(512, 256).astype(BF)
    turned[...] = mixed_ref[...].astype(F32).T.reshape(64, 2, 8, 256)
    left_p[0] = turned[:, c["core"]].reshape(512, 256).astype(BF)
    leave[1] = turned[:, 1 - c["core"]].reshape(512, 256).astype(BF)
    pl.semaphore_wait(barrier, len(partners))
    pair = [
        pltpu.make_async_remote_copy(
            src_ref=source,
            dst_ref=target,
            send_sem=pair_send.at[k],
            recv_sem=pair_recv.at[k],
            device_id=other,
            device_id_type=MESH,
        )
        for k, (source, target) in enumerate(
            (
                (leave.at[0], left_q.at[1]),
                (right_q.at[0], right_q.at[1]),
                (leave.at[1], left_p.at[1]),
                (right_p.at[0], right_p.at[1]),
            )
        )
    ]
    for copy in pair:
        copy.start()
    for copy in pair:
        copy.wait_recv()

    def product(left, right, columns):
        return jnp.dot(left[0], right[0, :, columns], preferred_element_type=F32) + jnp.dot(
            left[1], right[1, :, columns], preferred_element_type=F32
        )

    def tile(at):
        columns = pl.ds(at, 128)
        top = product(left_q, right_q, columns).reshape(64, 8, 128)
        if at < 1024:
            low = product(left_q, right_q, pl.ds(at + FOLD, 128))
        else:
            low = product(left_p, right_p, pl.ds(at - 1024, 128))
        both = jnp.concatenate([top, low.reshape(64, 8, 128)], axis=1)
        reducer.total[:, :, :, :, :, columns] = both.astype(BF).reshape(2, 4, 2, 4, 16, 128)

    for part in range(3):
        for at in range(PARTS[part][0], PARTS[part][1], 128):
            tile(at)
        reducer.start(part, 0)
    for step in range(2):
        for part in range(3):
            reducer.finish(part, step)
            reducer.start(part, step + 1)
    for part in range(3):
        store_folded(part, reducer.finish(part, 2), qkv_ref, proj_ref)
    for copy in pair:
        copy.wait_send()
    reducer.drain()


def weight_gradients(normed, grad_packed, mixed, grad_level):
    vmem = pl.BlockSpec(memory_space=pltpu.VMEM)
    return pl.pallas_call(
        weight_kernel,
        out_shape=(
            jax.ShapeDtypeStruct((8, 3072), F32),
            jax.ShapeDtypeStruct((8, 1024), F32),
        ),
        in_specs=[vmem] * 4,
        out_specs=(vmem, vmem),
        scratch_shapes=operand_scratch() + reduce_scratch(),
        compiler_params=pltpu.CompilerParams(
            collective_id=0, has_side_effects=True, vmem_limit_bytes=VMEM_LIMIT
        ),
    )(normed, grad_packed, mixed, grad_level)


def body(
    tokens, region, qkv_one, proj_one, merge_weight, qkv_two, proj_two, unmerge_weight, cotangent
):
    shifted = roll_forward(tokens)
    y_shift, back_one = jax.vjp(lambda field: level_one(field, region, qkv_one, proj_one), shifted)
    fine = roll_backward(y_shift)
    coarse, back_merge = jax.vjp(lambda field: merge_level(field, merge_weight), fine)
    row_tokens = gather_rows(coarse)
    width_two = row_tokens.shape[-1]
    normed_two = norm_rounded(row_tokens)
    packed_two = jnp.dot(normed_two, qkv_two, preferred_element_type=jnp.float32).astype(
        jnp.bfloat16
    )
    mixed_two, back_attend = jax.vjp(row_attention, packed_two)
    row_output = (
        row_tokens.astype(jnp.float32)
        + jnp.dot(mixed_two, proj_two, preferred_element_type=jnp.float32)
    ).astype(jnp.bfloat16)
    level_two = return_rows(row_output)
    upper, back_skip = jax.vjp(lambda field: skip_up(field, unmerge_weight), level_two)
    output = (fine.astype(jnp.float32) + upper).astype(jnp.bfloat16)
    (grad_level,) = back_skip(cotangent.astype(jnp.float32))
    grad_rowout = gather_rows(grad_level)
    flat_mixed = mixed_two.reshape(-1, width_two)
    grad_mixed = jnp.dot(grad_rowout, proj_two.T, preferred_element_type=jnp.float32).astype(
        jnp.bfloat16
    )
    (grad_packed,) = back_attend(grad_mixed)
    grad_qkv_two, grad_proj_two = weight_gradients(
        normed_two.reshape(-1, width_two),
        grad_packed.reshape(-1, 3 * width_two),
        flat_mixed,
        grad_rowout.reshape(-1, width_two),
    )
    grad_normed = jnp.dot(grad_packed, qkv_two.T, preferred_element_type=jnp.float32).astype(
        jnp.bfloat16
    )
    (grad_norm_in,) = jax.vjp(norm_rounded, row_tokens)[1](grad_normed)
    grad_rowin = (grad_rowout.astype(jnp.float32) + grad_norm_in.astype(jnp.float32)).astype(
        jnp.bfloat16
    )
    grad_coarse = return_rows(grad_rowin)
    (grad_merge_in,) = back_merge(grad_coarse)
    grad_fine = (cotangent.astype(jnp.float32) + grad_merge_in.astype(jnp.float32)).astype(
        jnp.bfloat16
    )
    grad_shift = roll_forward(grad_fine)
    (grad_shifted,) = back_one(grad_shift)
    grad_tokens = roll_backward(grad_shifted)
    return (output, grad_tokens, grad_qkv_two, grad_proj_two)


def solution(mesh):
    return jax.shard_map(
        body,
        mesh=mesh,
        in_specs=(
            P("lat", "lon", None),
            P("lat", "lon"),
            P(),
            P(),
            P(),
            P(),
            P(),
            P(),
            P("lat", "lon", None),
        ),
        out_specs=(
            P("lat", "lon", None),
            P("lat", "lon", None),
            P(("lat", "lon"), None),
            P(("lat", "lon"), None),
        ),
        check_vma=False,
    )
```

```python
import itertools
from types import SimpleNamespace

import jax
import jax.numpy as jnp
from jax import lax
from jax.experimental import pallas as pl
from jax.experimental.pallas import tpu as pltpu
from jax.sharding import PartitionSpec as P

MESH = pl.DeviceIdType.MESH
BF = jnp.bfloat16
F32 = jnp.float32
VMEM_LIMIT = 63 * 1024 * 1024

TOKENS, C1, C2 = 1024, 512, 1024
COARSE = 256
LONS, LATS = 16, 8

FOLD = 2048
PARTS = ((0, 640, ("x", "y", "z")), (640, 1280, ("y", "z", "x")), (1280, 2048, ("z", "x", "y")))
LABELS = ("zh", "x", "zl", "y")


def coordinates():
    lat, lon = lax.axis_index("lat"), lax.axis_index("lon")
    return {
        "zh": lat // 4,
        "x": lat % 4,
        "zl": lon // 8,
        "y": (lon // 2) % 4,
        "core": lon % 2,
    }


def device_of(c):
    return (c["zh"] * 4 + c["x"], (c["zl"] * 4 + c["y"]) * 2 + c["core"])


def moved(c, axis, by):
    c = dict(c)
    if axis == "z":
        z = (c["zh"] * 2 + c["zl"] + by) % 4
        c["zh"], c["zl"] = z // 2, z % 2
    elif axis == "core":
        c["core"] = 1 - c["core"]
    else:
        c[axis] = (c[axis] + by) % 4
    return c


def pick(labels, axis, c):
    names = ("zh", "zl") if axis == "z" else (axis,)
    return tuple(c[label] if label in names else slice(None) for label in labels)


def drop(labels, axis):
    names = ("zh", "zl") if axis == "z" else (axis,)
    return tuple(label for label in labels if label not in names)


def sizes(labels):
    return tuple(4 if label in ("x", "y") else 2 for label in labels)


def remote(source, target, send_sem, recv_sem, device):
    return pltpu.make_async_remote_copy(
        src_ref=source,
        dst_ref=target,
        send_sem=send_sem,
        recv_sem=recv_sem,
        device_id=device,
        device_id_type=MESH,
    )


def reduce_scratch():
    shapes = [pltpu.VMEM((2, 4, 2, 4, 16, FOLD), BF)]
    for start, stop, order in PARTS:
        labels = LABELS
        for step, axis in enumerate(order):
            labels = drop(labels, axis)
            shapes.append(pltpu.VMEM((3,) + sizes(labels) + (16, stop - start), BF))
            if step < 2:
                shapes.append(pltpu.VMEM(sizes(labels) + (16, stop - start), BF))
    return shapes + [pltpu.SemaphoreType.DMA((3, 3, 3)), pltpu.SemaphoreType.DMA((3, 3, 3))]


class Reducer:
    def __init__(self, scratch):
        self.total = scratch[0]
        self.slots = [scratch[1 + 5 * p : 6 + 5 * p] for p in range(3)]
        self.send_sem, self.recv_sem = scratch[16], scratch[17]
        self.c = coordinates()

    def source(self, part, step):
        start, stop, order = PARTS[part]
        labels = LABELS
        for axis in order[:step]:
            labels = drop(labels, axis)
        if step == 0:
            return labels, self.total, (slice(None), pl.ds(start, stop - start))
        return labels, self.slots[part][2 * step - 1], (slice(None), slice(None))

    def copies(self, part, step):
        axis = PARTS[part][2][step]
        labels, source, rest = self.source(part, step)
        found = []
        for by in (2, 1, 3):
            target = moved(self.c, axis, by)
            found.append(
                remote(
                    source.at[pick(labels, axis, target) + rest],
                    self.slots[part][2 * step].at[by - 1],
                    self.send_sem.at[part, step, by - 1],
                    self.recv_sem.at[part, step, by - 1],
                    device_of(target),
                )
            )
        return found

    def start(self, part, step):
        for copy in self.copies(part, step):
            copy.start()

    def finish(self, part, step):
        for copy in self.copies(part, step):
            copy.wait_recv()
        axis = PARTS[part][2][step]
        labels, source, rest = self.source(part, step)
        arrived = self.slots[part][2 * step]
        left = drop(labels, axis)
        for place in itertools.product(*[range(size) for size in sizes(left)]):
            where = dict(zip(left, place))
            where.update({k: self.c[k] for k in labels if k not in where})
            own = source[tuple(where[label] for label in labels) + rest].astype(F32)
            summed = own
            for slot in range(3):
                summed = summed + arrived[(slot,) + place].astype(F32)
            if step == 2:
                return summed
            self.slots[part][2 * step + 1][place] = summed.astype(BF)

    def drain(self):
        for part in range(3):
            for step in range(3):
                for copy in self.copies(part, step):
                    copy.wait_send()


def store_folded(part, summed, qkv_ref, proj_ref):
    start, stop, _ = PARTS[part]
    top, low = summed[:8], summed[8:]
    qkv_ref[:, start:stop] = top
    cut = min(max(1024 - start, 0), stop - start)
    if cut:
        qkv_ref[:, FOLD + start : FOLD + start + cut] = low[:, :cut]
    if cut < stop - start:
        proj_ref[:, start + cut - 1024 : stop - 1024] = low[:, cut:]


def block(at, size):
    return pl.ds(pl.multiple_of(at * size, size), size)


def loop(count, body):
    def step(at, carry):
        body(at)
        return carry

    lax.fori_loop(0, count, step, 0)


def dot(a, b):
    return jnp.dot(a, b, preferred_element_type=F32)


def dot_nt(a, b):
    return lax.dot_general(a, b, (((1,), (1,)), ((), ())), preferred_element_type=F32)


def dot_tn(a, b):
    return lax.dot_general(a, b, (((0,), (0,)), ((), ())), preferred_element_type=F32)


def normalised(x):
    centered = x - jnp.mean(x, axis=-1, keepdims=True)
    spread = jnp.mean(centered * centered, axis=-1, keepdims=True)
    scale = lax.rsqrt(spread + 1e-05)
    return centered * scale, scale


def norm_back(x, g):
    hat, scale = normalised(x)
    return scale * (
        g - jnp.mean(g, axis=-1, keepdims=True) - hat * jnp.mean(g * hat, axis=-1, keepdims=True)
    )


def by_head(pair, scale=1.0):
    lane = lax.broadcasted_iota(jnp.int32, (1, 128), 1)
    first = jnp.where(lane < 64, scale, 0.0).astype(BF)
    second = jnp.where(lane < 64, 0.0, scale).astype(BF)
    return jnp.concatenate([pair * first, pair * second], axis=0)


def side_by_side(stacked):
    return jnp.concatenate([stacked[:128], stacked[128:]], axis=1)


def attend(units, allowed):
    ones = by_head(jnp.ones((128, 128), BF))
    scores = [dot_nt(by_head(q, 0.125), k) for q, k, _ in units]
    if allowed is not None:
        scores = [
            jnp.where(allowed[None], one.reshape(2, 128, 128), -1e30).reshape(256, 128)
            for one in scores
        ]
    expo = [jnp.exp(one - jnp.max(one, axis=-1, keepdims=True)).astype(BF) for one in scores]
    found = []
    for one, (_, _, v) in zip(expo, units):
        both = dot(side_by_side(one), jnp.concatenate([by_head(v), ones], axis=1))
        over = 1.0 / both[:, 128:]
        found.append((one, over.astype(BF), (both[:, :128] * over).astype(BF)))
    return found


def attend_back(units):
    minus = jnp.full((128, 128), -1.0, BF)
    found = []
    for q, k, v, expo, over, mixed, g in units:
        g = g * over
        both = by_head(g)
        change = dot_nt(
            jnp.concatenate([both, by_head(g * mixed)], axis=1),
            jnp.concatenate([v, minus], axis=1),
        )
        grad_scores = (expo.astype(F32) * change).astype(BF)
        grad_q = dot(side_by_side(grad_scores), by_head(k, 0.125))
        grad_k = dot_tn(grad_scores, by_head(q, 0.125))
        grad_v = dot_tn(expo, both)
        found.append((grad_q.astype(BF), grad_k.astype(BF), grad_v.astype(BF)))
    return found


def pack_columns(rows):
    n = rows.shape[0] // 32
    width = rows.shape[1]
    late = rows.reshape(n, 2, 16, width)[:, :, 8:, :]
    place = lax.broadcasted_iota(jnp.int32, (n, 8, width), 1)
    both = jnp.where(place < 4, pltpu.roll(late[:, 0], 4, 1), late[:, 1])
    return both.reshape(n * 8, width).astype(BF)


def put_columns(rows, packed):
    n = rows.shape[0] // 32
    width = rows.shape[1]
    pairs = rows.reshape(n, 2, 16, width)
    arrived = packed.astype(F32).reshape(n, 8, width)
    place = lax.broadcasted_iota(jnp.int32, (n, 8, width), 1)
    even = jnp.where(place >= 4, pltpu.roll(arrived, 4, 1), pairs[:, 0, 8:])
    odd = jnp.where(place >= 4, arrived, pairs[:, 1, 8:])
    whole = jnp.concatenate([pairs[:, 0, :8], even, pairs[:, 1, :8], odd], axis=1)
    return whole.reshape(n * 32, width)


class Halo:

    def __init__(self, field, scratch, way, start=0):
        self.field, self.first = field, start
        self.packed, self.columns, self.rows, self.send_sem, self.recv_sem = scratch
        self.way = way

    def pack(self, half):
        def body(at):
            at = at + 4 * half
            rows = self.field[pl.ds(pl.multiple_of(at * 128 + self.first, 64), 128)]
            self.packed[block(at, 32)] = pack_columns(rows.astype(F32))

        loop(4, body)

    def copies(self):
        lat, lon = lax.axis_index("lat"), lax.axis_index("lon")
        way = self.way
        lat_to, lon_to = (lat + way) % LATS, (lon + way) % LONS
        if way == 1:
            plan = (
                (self.field.at[self.first + 960 : self.first + 1024], self.rows.at[:], (lat_to, lon)),
                (self.packed.at[240:256], self.columns.at[0:16], (lat_to, lon_to)),
                (self.packed.at[0:128], self.columns.at[16:144], (lat, lon_to)),
                (self.packed.at[128:240], self.columns.at[144:256], (lat, lon_to)),
            )
        else:
            plan = (
                (self.field.at[0:64], self.rows.at[:], (lat_to, lon)),
                (self.packed.at[0:16], self.columns.at[240:256], (lat_to, lon_to)),
                (self.packed.at[16:128], self.columns.at[0:112], (lat, lon_to)),
                (self.packed.at[128:256], self.columns.at[112:240], (lat, lon_to)),
            )
        return [
            remote(source, target, self.send_sem.at[k], self.recv_sem.at[k], device)
            for k, (source, target, device) in enumerate(plan)
        ]

    def start(self, which):
        copies = self.copies()
        for k in which:
            copies[k].start()

    def wait(self, which):
        copies = self.copies()
        for k in which:
            copies[k].wait_recv()

    def drain(self):
        for copy in self.copies():
            copy.wait_send()

    def assemble(self, part, write):
        if self.way == 1:
            if part == 0:
                write(0, put_columns(self.rows[...].astype(F32), self.columns[0:16]))

            def patch(at):
                at = at + 8 * part
                rows = self.field[pl.ds(pl.multiple_of(at * 64 + self.first, 64), 64)]
                write(at + 1, put_columns(rows.astype(F32), self.columns[block(at + 1, 16)]))

            loop(7 if part else 8, patch)
        else:
            if part == 0:
                write(15, put_columns(self.rows[...].astype(F32), self.columns[240:256]))

            def patch(at):
                at = at + 7 * part
                rows = self.field[block(at + 1, 64)]
                write(at, put_columns(rows.astype(F32), self.columns[block(at, 16)]))

            loop(8 if part else 7, patch)


def halo_scratch():
    return [
        pltpu.VMEM((256, C1), BF),
        pltpu.VMEM((256, C1), BF),
        pltpu.VMEM((64, C1), BF),
        pltpu.SemaphoreType.DMA((4,)),
        pltpu.SemaphoreType.DMA((4,)),
    ]


class Rows:

    def __init__(self, source, target, sems):
        self.source, self.target = source, target
        self.send_sem, self.recv_sem = sems

    def copy(self, by):
        lat, lon = lax.axis_index("lat"), lax.axis_index("lon")
        to = (lon + by) % LONS
        return remote(
            self.source.at[block(to, 16)],
            self.target.at[block(lon, 16)],
            self.send_sem.at[by],
            self.recv_sem.at[by],
            (lat, to),
        )

    def start(self):
        loop(15, lambda at: self.copy(at + 1).start())
        lon = lax.axis_index("lon")
        self.target[block(lon, 16)] = self.source[block(lon, 16)]

    def wait(self):
        loop(15, lambda at: self.copy(at + 1).wait_recv())

    def drain(self):
        loop(15, lambda at: self.copy(at + 1).wait_send())


def spread_lanes(ref, at, rows):
    for k in range(4):
        ref[k, block(at, 64)] = rows[:, 128 * k : 128 * k + 128]


def fine_pieces(ref, at):
    found = {}
    for b in range(2):
        lanes = [ref[k, pl.ds(at * 64 + b, 32, 2), :] for k in range(4)]
        rows = jnp.concatenate(lanes, axis=1).reshape(2, 2, 8, C1)
        for a in range(2):
            found[a, b] = rows[:, a].reshape(16, C1)
    return [found[a, b] for a in range(2) for b in range(2)]


def put_pieces(ref, at, pieces):
    for b in range(2):
        rows = jnp.stack(
            [pieces[b].reshape(2, 8, C1), pieces[2 + b].reshape(2, 8, C1)], axis=1
        ).reshape(32, C1)
        for k in range(4):
            ref[k, pl.ds(at * 64 + b, 32, 2), :] = rows[:, 128 * k : 128 * k + 128]


def joined_rows(ref, at, width):
    return jnp.concatenate([ref[k, block(at, 64)] for k in range(4)], axis=1)


def by_row(x, width):
    x = x.reshape(-1, 2, 8, width)
    return x[:, 0], x[:, 1]


WEIGHTS = dict(
    unmerge=(C2, 4 * C1),
    qkv_one=(C1, 3 * C1),
    proj_one=(C1, C1),
    merge=(4 * C1, C2),
    qkv_two=(C2, 3 * C2),
    proj_two=(C2, C2),
)

BUFFERS = dict(
    window=((TOKENS + 64, C1), BF),
    labels=((8, 128), F32),
    normed_one=((TOKENS, C1), BF),
    packed_one=((TOKENS, 3 * C1), BF),
    expo_one=((32, 256, 128), BF),
    over_one=((32, 128, 128), BF),
    mixed_one=((TOKENS, C1), BF),
    y_shift=((TOKENS, C1), BF),
    grads=((TOKENS, C1), BF),
    outgoing=((TOKENS, C1), BF),
    fine=((COARSE, 4 * C1), BF),
    spare=((4, TOKENS, 128), F32),
    grouped=((COARSE, 4 * C1), BF),
    coarse=((COARSE, C2), BF),
    coarse_rows=((COARSE, C2), BF),
    grad_skip=((COARSE, C2), BF),
    grad_skip_rows=((COARSE, C2), BF),
    normed_two=((COARSE, C2), BF),
    packed_two=((COARSE, 3 * C2), BF),
    expo_two=((16, 256, 128), BF),
    over_two=((16, 128, 128), BF),
    mixed_two=((COARSE, C2), BF),
    grad_mixed_two=((COARSE, C2), BF),
    wide=((COARSE, C2), F32),
    level_two_rows=((COARSE, C2), BF),
    level_two=((COARSE, C2), BF),
    grad_coarse_rows=((COARSE, C2), BF),
    grad_coarse=((COARSE, C2), BF),
    left_q=((512, 512), BF),
    left_p=((512, 512), BF),
    leave=((2, 512, 256), BF),
    right_q=((2 * COARSE, 3 * C2), BF),
    right_p=((2 * COARSE, C2), BF),
)


def scratch_list():
    shapes = [pltpu.VMEM(shape, BF) for shape in WEIGHTS.values()]
    shapes += [pltpu.VMEM(shape, dtype) for shape, dtype in BUFFERS.values()]
    shapes += [pltpu.SemaphoreType.DMA((len(WEIGHTS),)), pltpu.SemaphoreType.DMA((5,))]
    shapes += [pltpu.SemaphoreType.DMA((4,)), pltpu.SemaphoreType.DMA((4,))]
    shapes += [pltpu.SemaphoreType.DMA((LONS,)) for _ in range(8)]
    for _ in range(4):
        shapes += halo_scratch()
    return shapes + reduce_scratch()


def whole_kernel(*refs):
    region, tokens, cotangent = refs[:3]
    stored = refs[3:9]
    out_ref, grad_ref, qkv_ref, proj_ref = refs[9:13]
    scratch = list(refs[13:])

    def take(count):
        taken = scratch[:count]
        del scratch[:count]
        return taken

    weight = SimpleNamespace(**dict(zip(WEIGHTS, take(len(WEIGHTS)))))
    buf = SimpleNamespace(**dict(zip(BUFFERS, take(len(BUFFERS)))))
    load_sem, field_sem = take(2)
    pair_send, pair_recv = take(2)
    row_sems = [take(2) for _ in range(4)]
    halos = [take(5) for _ in range(4)]
    reducer = Reducer(take(len(reduce_scratch())))
    c = reducer.c
    lat, lon = lax.axis_index("lat"), lax.axis_index("lon")

    partners = [(lat, (lon + by) % LONS) for by in range(1, LONS)]
    for way in (1, -1):
        partners.append(((lat + way) % LATS, lon))
        partners.append(((lat + way) % LATS, (lon + way) % LONS))
    partners += [device_of(moved(c, axis, by)) for axis in ("x", "y", "z") for by in (1, 2, 3)]
    barrier = pltpu.get_barrier_semaphore()
    for partner in partners:
        pl.semaphore_signal(barrier, inc=1, device_id=partner, device_id_type=MESH)

    loads = {
        name: pltpu.make_async_copy(source, getattr(weight, name), load_sem.at[k])
        for k, (name, source) in enumerate(zip(WEIGHTS, stored))
    }
    token_load = pltpu.make_async_copy(tokens, buf.window.at[64:1088], field_sem.at[0])
    cotangent_load = pltpu.make_async_copy(cotangent, buf.mixed_one, field_sem.at[1])
    cotangent_again = pltpu.make_async_copy(cotangent, buf.y_shift, field_sem.at[2])
    output_store = pltpu.make_async_copy(buf.outgoing, out_ref, field_sem.at[3])
    grad_store = pltpu.make_async_copy(buf.outgoing, grad_ref, field_sem.at[4])
    token_load.start()
    cotangent_load.start()
    for copy in loads.values():
        copy.start()
    loads = SimpleNamespace(**loads)

    column = lax.broadcasted_iota(jnp.int32, (16, 128), 0)
    place = lax.broadcasted_iota(jnp.int32, (16, 128), 1) & 15
    chosen = jnp.where(column == ((place + 4) & 15), 1.0, 0.0).astype(BF)
    spread_region = dot_tn(region[...].astype(F32).astype(BF), chosen).reshape(8, 8, 128)
    row = lax.broadcasted_iota(jnp.int32, (8, 8, 128), 1)
    token = lax.broadcasted_iota(jnp.int32, (8, 8, 128), 2)
    own_row = jnp.where(row == (token >> 4), spread_region, 0.0)
    second = jnp.where(((token + 4) & 15) >= 8, 1.0, 0.0)[:, 0]
    buf.labels[...] = jnp.sum(own_row, axis=1) * 2.0 + second

    tokens_in = Halo(buf.window, halos[0], 1, 64)
    fine_back = Halo(buf.y_shift, halos[1], -1)
    grads_in = Halo(buf.normed_one, halos[2], 1)
    grads_back = Halo(buf.y_shift, halos[3], -1)
    skip_to_rows = Rows(buf.grad_skip, buf.grad_skip_rows, row_sems[0])
    coarse_to_rows = Rows(buf.coarse, buf.coarse_rows, row_sems[1])
    level_to_tile = Rows(buf.level_two_rows, buf.level_two, row_sems[2])
    grad_to_tile = Rows(buf.grad_coarse_rows, buf.grad_coarse, row_sems[3])

    with jax.named_scope("tokens_in"):
        token_load.wait()
        tokens_in.pack(0)
        tokens_in.pack(1)
        pl.semaphore_wait(barrier, len(partners))
        tokens_in.start(range(4))

    with jax.named_scope("grad_skip"):
        cotangent_load.wait()

        def spread(at):
            spread_lanes(buf.spare, at, buf.mixed_one[block(at, 64)].astype(F32))

        loop(16, spread)

        def group_cotangent(at):
            buf.grouped[block(at, 16)] = jnp.concatenate(
                fine_pieces(buf.spare, at), axis=1
            ).astype(BF)

        loop(16, group_cotangent)
        loads.unmerge.wait()

        def grad_skip(at):
            buf.grad_skip[:, block(at, 256)] = dot_nt(
                buf.grouped[...], weight.unmerge[block(at, 256)]
            ).astype(BF)

        loop(4, grad_skip)
        skip_to_rows.start()

    def lanes(third, pair):
        return slice(C1 * third + 128 * pair, C1 * third + 128 * pair + 128)

    def windows_allowed(group):
        row = jnp.broadcast_to(buf.labels[pl.ds(group, 1), :], (128, 128))
        return row == row.T

    with jax.named_scope("level_one"):
        def write_window(at, rows):
            buf.window[block(at, 64)] = rows.astype(BF)
            buf.normed_one[block(at, 64)] = normalised(rows)[0].astype(BF)

        loads.qkv_one.wait()
        loads.proj_one.wait()
        for half in range(2):
            tokens_in.wait((3,) if half else (0, 1, 2))
            tokens_in.assemble(half, write_window)
            rows = slice(512 * half, 512 * half + 512)

            def project(at):
                buf.packed_one[rows, block(at, 256)] = dot(
                    buf.normed_one[rows], weight.qkv_one[:, block(at, 256)]
                ).astype(BF)

            loop(6, project)

            def attend_group(at):
                group = at + 4 * half
                where = block(group, 128)
                units = [
                    [buf.packed_one[where, lanes(third, pair)] for third in range(3)]
                    for pair in range(4)
                ]
                for pair, found in enumerate(attend(units, windows_allowed(group))):
                    at_unit = group * 4 + pair
                    buf.expo_one[at_unit], buf.over_one[at_unit], mixed = found
                    buf.mixed_one[where, lanes(0, pair)] = mixed

            loop(4, attend_group)

            def add_tokens(at):
                columns = block(at, 256)
                buf.y_shift[rows, columns] = (
                    buf.window[rows, columns].astype(F32)
                    + dot(buf.mixed_one[rows], weight.proj_one[:, columns])
                ).astype(BF)

            loop(2, add_tokens)
            fine_back.pack(half)
            fine_back.start((0, 1, 2) if half == 0 else (3,))

    with jax.named_scope("merge"):
        def write_fine(at, rows):
            spread_lanes(buf.spare, at, rows.astype(BF).astype(F32))

        fine_back.wait((0, 1, 2))
        fine_back.assemble(0, write_fine)
        fine_back.wait((3,))
        fine_back.assemble(1, write_fine)

        def group_fine(at):
            whole = jnp.concatenate(fine_pieces(buf.spare, at), axis=1)
            buf.fine[block(at, 16)] = whole.astype(BF)
            buf.grouped[block(at, 16)] = normalised(whole)[0].astype(BF)

        loop(16, group_fine)
        loads.merge.wait()

        def merge(at):
            columns = block(at, 256)
            buf.coarse[:, columns] = dot(
                buf.grouped[...], weight.merge[:, columns]
            ).astype(BF)

        loop(4, merge)
        coarse_to_rows.start()
        fine_back.drain()
        cotangent_again.start()

    with jax.named_scope("level_two"):
        loads.qkv_two.wait()
        loads.proj_two.wait()
        coarse_to_rows.wait()

        def norm_two(at):
            both = by_row(buf.coarse_rows[block(at, 64)].astype(F32), C2)
            for row in range(2):
                x = both[row].reshape(32, C2)
                where = pl.ds(pl.multiple_of(at * 32 + 128 * row, 32), 32)
                buf.wide[where] = x
                buf.normed_two[where] = normalised(x)[0].astype(BF)

        loop(4, norm_two)

        def project_two(at):
            columns = block(at, 256)
            buf.packed_two[:, columns] = dot(
                buf.normed_two[...], weight.qkv_two[:, columns]
            ).astype(BF)

        loop(12, project_two)

        def operands_two(row, pair):
            rows = slice(128 * row, 128 * row + 128)
            return [
                buf.packed_two[rows, pl.ds(pl.multiple_of(C2 * third + pair * 128, 128), 128)]
                for third in range(3)
            ]

        def attend_two(at):
            places = [(2 * at + k, row) for k in range(2) for row in range(2)]
            units = [operands_two(row, pair) for pair, row in places]
            for (pair, row), found in zip(places, attend(units, None)):
                at_unit = pair * 2 + row
                buf.expo_two[at_unit], buf.over_two[at_unit], mixed = found
                buf.mixed_two[128 * row : 128 * row + 128, block(pair, 128)] = mixed

        loop(4, attend_two)

        def add_coarse(at):
            columns = block(at, 256)
            total = buf.wide[:, columns] + dot(buf.mixed_two[...], weight.proj_two[:, columns])
            buf.level_two_rows[:, columns] = (
                jnp.stack([total[:128].reshape(16, 8, 256), total[128:].reshape(16, 8, 256)], axis=1)
                .reshape(256, 256)
                .astype(BF)
            )

        loop(4, add_coarse)
        level_to_tile.start()

    with jax.named_scope("grad_level_two"):
        skip_to_rows.wait()

        def grad_level(at):
            x = buf.level_two_rows[block(at, 64)].astype(F32)
            g = buf.grad_skip_rows[block(at, 64)].astype(F32)
            both = by_row(norm_back(x, g), C2)
            for row in range(2):
                where = pl.ds(pl.multiple_of(at * 32 + 128 * row, 32), 32)
                buf.right_p[where] = both[row].reshape(32, C2).astype(BF)

        loop(4, grad_level)

        def grad_mixed(at):
            buf.grad_mixed_two[:, block(at, 256)] = dot_nt(
                buf.right_p[0:256], weight.proj_two[block(at, 256)]
            ).astype(BF)

        loop(4, grad_mixed)

        def attend_two_back(at):
            places = [(2 * at + k, row) for k in range(2) for row in range(2)]
            units = []
            for pair, row in places:
                rows = slice(128 * row, 128 * row + 128)
                units.append(
                    operands_two(row, pair)
                    + [
                        buf.expo_two[pair * 2 + row],
                        buf.over_two[pair * 2 + row],
                        buf.mixed_two[rows, block(pair, 128)],
                        buf.grad_mixed_two[rows, block(pair, 128)],
                    ]
                )
            for (pair, row), found in zip(places, attend_back(units)):
                for third in range(3):
                    where = pl.ds(pl.multiple_of(C2 * third + pair * 128, 128), 128)
                    buf.right_q[128 * row : 128 * row + 128, where] = found[third]

        loop(4, attend_two_back)

    def turn(source, left, slot):
        first = c["core"] == 0
        for half in range(2):
            tokens_at = slice(128 * half, 128 * half + 128)
            groups = source[tokens_at].astype(F32).T.reshape(64, 2, 8, 128)
            mine = jnp.where(first, groups[:, 0], groups[:, 1])
            theirs = jnp.where(first, groups[:, 1], groups[:, 0])
            left[:, tokens_at] = mine.reshape(512, 128).astype(BF)
            buf.leave[slot, :, tokens_at] = theirs.reshape(512, 128).astype(BF)

    pair_copies = [
        remote(source, target, pair_send.at[k], pair_recv.at[k], device_of(moved(c, "core", 1)))
        for k, (source, target) in enumerate(
            (
                (buf.right_q.at[0:256], buf.right_q.at[256:512]),
                (buf.right_p.at[0:256], buf.right_p.at[256:512]),
                (buf.leave.at[0], buf.left_q.at[:, 256:512]),
                (buf.leave.at[1], buf.left_p.at[:, 256:512]),
            )
        )
    ]

    with jax.named_scope("grad_coarse"):
        pair_copies[0].start()
        pair_copies[1].start()

        def grad_normed_two(at):
            buf.grad_mixed_two[:, block(at, 256)] = dot_nt(
                buf.right_q[0:256], weight.qkv_two[block(at, 256)]
            ).astype(BF)

        loop(4, grad_normed_two)

        def grad_coarse(at):
            both = []
            for row in range(2):
                where = pl.ds(pl.multiple_of(at * 32 + 128 * row, 32), 32)
                g = norm_back(buf.wide[where], buf.grad_mixed_two[where].astype(F32))
                g = g.astype(BF).astype(F32) + buf.right_p[where].astype(F32)
                both.append(g.reshape(4, 8, C2))
            buf.grad_coarse_rows[block(at, 64)] = (
                jnp.stack(both, axis=1).reshape(64, C2).astype(BF)
            )

        loop(4, grad_coarse)
        grad_to_tile.start()

    with jax.named_scope("weight_gradients"):
        turn(buf.normed_two, buf.left_q, 0)
        pair_copies[2].start()
        turn(buf.mixed_two, buf.left_p, 1)
        pair_copies[3].start()
        for copy in pair_copies:
            copy.wait_recv()

        def put_total(zh, columns, top, low):
            width = top.shape[1]
            both = jnp.concatenate([top.reshape(32, 8, width), low.reshape(32, 8, width)], axis=1)
            reducer.total[zh, :, :, :, :, columns] = both.astype(BF).reshape(4, 2, 4, 16, width)

        def narrow_tile(at):
            right = jnp.concatenate(
                [buf.right_q[:, block(at, 128)], buf.right_q[:, block(at + 16, 128)]], axis=1
            )
            for zh in range(2):
                both = dot(buf.left_q[256 * zh : 256 * zh + 256], right)
                put_total(zh, block(at, 128), both[:, :128], both[:, 128:])

        def wide_tile(at):
            for zh in range(2):
                rows = slice(256 * zh, 256 * zh + 256)
                top = dot(buf.left_q[rows], buf.right_q[:, block(at, 256)])
                low = dot(buf.left_p[rows], buf.right_p[:, block(at - 4, 256)])
                put_total(zh, block(at, 256), top, low)

        for part, (start, stop, _) in enumerate(PARTS):
            middle = max(start, min(stop, 1024))
            if middle > start:
                loop((middle - start) // 128, lambda at: narrow_tile(at + start // 128))
            if stop > middle:
                loop((stop - middle) // 256, lambda at: wide_tile(at + middle // 256))
            reducer.start(part, 0)

    with jax.named_scope("grad_fine"):
        grad_to_tile.wait()

        def grad_grouped(at):
            buf.grouped[:, block(at, 256)] = dot_nt(
                buf.grad_coarse[...], weight.merge[block(at, 256)]
            ).astype(BF)

        loop(8, grad_grouped)

        def grad_pieces(at):
            g = norm_back(
                buf.fine[block(at, 16)].astype(F32), buf.grouped[block(at, 16)].astype(F32)
            )
            put_pieces(buf.spare, at, [g[:, C1 * k : C1 * k + C1] for k in range(4)])

        loop(16, grad_pieces)

        cotangent_again.wait()

        def grad_fine(at):
            buf.normed_one[block(at, 64)] = (
                joined_rows(buf.spare, at, C1) + buf.y_shift[block(at, 64)].astype(F32)
            ).astype(BF)

        loop(16, grad_fine)
        grads_in.pack(0)
        grads_in.pack(1)
        grads_in.start(range(4))

    with jax.named_scope("output"):
        level_to_tile.wait()

        def norm_level(at):
            x = buf.level_two[block(at, 64)].astype(F32)
            buf.coarse[block(at, 64)] = normalised(x)[0].astype(BF)

        coarse_to_rows.drain()
        loop(4, norm_level)

        for half in range(2):
            rows = slice(128 * half, 128 * half + 128)

            def unmerge(at):
                for low in range(2):
                    buf.wide[128 * low : 128 * low + 128, block(at, 256)] = dot(
                        buf.coarse[rows], weight.unmerge[:, block(at + 4 * low, 256)]
                    )

            loop(4, unmerge)

            def add_fine(at):
                fine = buf.fine[block(at + 8 * half, 16)].astype(F32)
                upper = jnp.concatenate(
                    [buf.wide[block(at, 16)], buf.wide[block(at + 8, 16)]], axis=1
                )
                total = fine + upper
                put_pieces(
                    buf.spare,
                    at + 8 * half,
                    [total[:, C1 * k : C1 * k + C1] for k in range(4)],
                )

            loop(8, add_fine)

        def write_output(at):
            buf.outgoing[block(at, 64)] = joined_rows(buf.spare, at, C1).astype(BF)

        loop(16, write_output)
        output_store.start()

    with jax.named_scope("grad_level_one"):

        def write_grads(at, rows):
            buf.grads[block(at, 64)] = rows.astype(BF)

        grads_in.wait(range(4))
        grads_in.assemble(0, write_grads)
        grads_in.assemble(1, write_grads)
        grads_in.drain()
        for half in range(2):
            rows = slice(512 * half, 512 * half + 512)

            def grad_mixed_one(at):
                buf.normed_one[rows, block(at, 256)] = dot_nt(
                    buf.grads[rows], weight.proj_one[block(at, 256)]
                ).astype(BF)

            loop(2, grad_mixed_one)

            def attend_group_back(at):
                group = at + 4 * half
                where = block(group, 128)
                units = []
                for pair in range(4):
                    at_unit = group * 4 + pair
                    units.append(
                        [buf.packed_one[where, lanes(third, pair)] for third in range(3)]
                        + [
                            buf.expo_one[at_unit],
                            buf.over_one[at_unit],
                            buf.mixed_one[where, lanes(0, pair)],
                            buf.normed_one[where, lanes(0, pair)],
                        ]
                    )
                for pair, found in enumerate(attend_back(units)):
                    for third in range(3):
                        buf.packed_one[where, lanes(third, pair)] = found[third]

            loop(4, attend_group_back)

            def grad_normed_one(at):
                buf.normed_one[rows, block(at, 256)] = dot_nt(
                    buf.packed_one[rows], weight.qkv_one[block(at, 256)]
                ).astype(BF)

            loop(2, grad_normed_one)

            def grad_window(at):
                where = block(at + 8 * half, 64)
                g = norm_back(
                    buf.window[where].astype(F32), buf.normed_one[where].astype(F32)
                )
                buf.y_shift[where] = (g + buf.grads[where].astype(F32)).astype(BF)

            loop(8, grad_window)
            grads_back.pack(half)
            grads_back.start((0, 1, 2) if half == 0 else (3,))
            for part in range(3):
                reducer.finish(part, half)
                reducer.start(part, half + 1)

    with jax.named_scope("grad_tokens"):
        output_store.wait()

        def write_tokens(at, rows):
            buf.outgoing[block(at, 64)] = rows.astype(BF)

        grads_back.wait((0, 1, 2))
        grads_back.assemble(0, write_tokens)
        grads_back.wait((3,))
        grads_back.assemble(1, write_tokens)
        grad_store.start()
        for part in range(3):
            store_folded(part, reducer.finish(part, 2), qkv_ref, proj_ref)

    tokens_in.drain()
    grads_back.drain()
    skip_to_rows.drain()
    level_to_tile.drain()
    grad_to_tile.drain()
    for copy in pair_copies:
        copy.wait_send()
    reducer.drain()
    grad_store.wait()


def hand_over(*refs):
    for source, target in zip(refs[:4], refs[4:]):
        target[...] = source[...]


def body(
    tokens, region, qkv_one, proj_one, merge_weight, qkv_two, proj_two, unmerge_weight, cotangent
):
    vmem = pl.BlockSpec(memory_space=pltpu.VMEM)
    anywhere = pl.BlockSpec(memory_space=pl.ANY)
    shapes = (
            jax.ShapeDtypeStruct((TOKENS, C1), BF),
            jax.ShapeDtypeStruct((TOKENS, C1), BF),
            jax.ShapeDtypeStruct((8, 3 * C2), F32),
            jax.ShapeDtypeStruct((8, C2), F32),
    )
    found = pl.pallas_call(
        whole_kernel,
        out_shape=shapes,
        in_specs=[vmem] + [anywhere] * 8,
        out_specs=(anywhere, anywhere, vmem, vmem),
        scratch_shapes=scratch_list(),
        compiler_params=pltpu.CompilerParams(
            collective_id=0, has_side_effects=True, vmem_limit_bytes=VMEM_LIMIT
        ),
    )(
        region.T,
        tokens.reshape(TOKENS, C1),
        cotangent.reshape(TOKENS, C1),
        unmerge_weight,
        qkv_one,
        proj_one,
        merge_weight,
        qkv_two,
        proj_two,
    )
    pieces = [
        pl.BlockSpec((TOKENS // 4, C1), lambda at: (at, 0)),
        pl.BlockSpec((TOKENS // 4, C1), lambda at: (at, 0)),
        pl.BlockSpec((8, 3 * C2 // 4), lambda at: (0, at)),
        pl.BlockSpec((8, C2 // 4), lambda at: (0, at)),
    ]
    output, grad_tokens, grad_qkv_two, grad_proj_two = pl.pallas_call(
        hand_over, grid=(4,), out_shape=shapes, in_specs=pieces, out_specs=pieces
    )(*found)
    shape = tokens.shape
    return output.reshape(shape), grad_tokens.reshape(shape), grad_qkv_two, grad_proj_two


def solution(mesh):
    return jax.shard_map(
        body,
        mesh=mesh,
        in_specs=(
            P("lat", "lon", None),
            P("lat", "lon"),
            P(),
            P(),
            P(),
            P(),
            P(),
            P(),
            P("lat", "lon", None),
        ),
        out_specs=(
            P("lat", "lon", None),
            P("lat", "lon", None),
            P(("lat", "lon"), None),
            P(("lat", "lon"), None),
        ),
        check_vma=False,
    )
```

```python
import itertools
from types import SimpleNamespace

import jax
import jax.numpy as jnp
from jax import lax
from jax.experimental import pallas as pl
from jax.experimental.pallas import tpu as pltpu
from jax.sharding import PartitionSpec as P

MESH = pl.DeviceIdType.MESH
BF = jnp.bfloat16
F32 = jnp.float32
VMEM_LIMIT = 63 * 1024 * 1024

TOKENS, C1, C2 = 1024, 512, 1024
COARSE = 256
LONS, LATS = 16, 8
DENSE, HEADS, TILES = 4, 1, 1

FOLD = 2048
PARTS = ((0, 640, ("x", "y", "z")), (640, 1280, ("y", "z", "x")), (1280, 2048, ("z", "x", "y")))
LABELS = ("zh", "x", "zl", "y")


def coordinates():
    lat, lon = lax.axis_index("lat"), lax.axis_index("lon")
    return {
        "zh": lat // 4,
        "x": lat % 4,
        "zl": lon // 8,
        "y": (lon // 2) % 4,
        "core": lon % 2,
    }


def device_of(c):
    return (c["zh"] * 4 + c["x"], (c["zl"] * 4 + c["y"]) * 2 + c["core"])


def moved(c, axis, by):
    c = dict(c)
    if axis == "z":
        z = (c["zh"] * 2 + c["zl"] + by) % 4
        c["zh"], c["zl"] = z // 2, z % 2
    elif axis == "core":
        c["core"] = 1 - c["core"]
    else:
        c[axis] = (c[axis] + by) % 4
    return c


def pick(labels, axis, c):
    names = ("zh", "zl") if axis == "z" else (axis,)
    return tuple(c[label] if label in names else slice(None) for label in labels)


def drop(labels, axis):
    names = ("zh", "zl") if axis == "z" else (axis,)
    return tuple(label for label in labels if label not in names)


def sizes(labels):
    return tuple(4 if label in ("x", "y") else 2 for label in labels)


def remote(source, target, send_sem, recv_sem, device):
    return pltpu.make_async_remote_copy(
        src_ref=source,
        dst_ref=target,
        send_sem=send_sem,
        recv_sem=recv_sem,
        device_id=device,
        device_id_type=MESH,
    )


def reduce_scratch():
    shapes = [pltpu.VMEM((2, 4, 2, 4, 16, FOLD), BF)]
    for start, stop, order in PARTS:
        labels = LABELS
        for step, axis in enumerate(order):
            labels = drop(labels, axis)
            shapes.append(pltpu.VMEM((3,) + sizes(labels) + (16, stop - start), BF))
            if step < 2:
                shapes.append(pltpu.VMEM(sizes(labels) + (16, stop - start), BF))
    return shapes + [pltpu.SemaphoreType.DMA((3, 3, 3)), pltpu.SemaphoreType.DMA((3, 3, 3))]


class Reducer:
    def __init__(self, scratch):
        self.total = scratch[0]
        self.slots = [scratch[1 + 5 * p : 6 + 5 * p] for p in range(3)]
        self.send_sem, self.recv_sem = scratch[16], scratch[17]
        self.c = coordinates()

    def source(self, part, step):
        start, stop, order = PARTS[part]
        labels = LABELS
        for axis in order[:step]:
            labels = drop(labels, axis)
        if step == 0:
            return labels, self.total, (slice(None), pl.ds(start, stop - start))
        return labels, self.slots[part][2 * step - 1], (slice(None), slice(None))

    def copies(self, part, step):
        axis = PARTS[part][2][step]
        labels, source, rest = self.source(part, step)
        found = []
        for by in (2, 1, 3):
            target = moved(self.c, axis, by)
            found.append(
                remote(
                    source.at[pick(labels, axis, target) + rest],
                    self.slots[part][2 * step].at[by - 1],
                    self.send_sem.at[part, step, by - 1],
                    self.recv_sem.at[part, step, by - 1],
                    device_of(target),
                )
            )
        return found

    def start(self, part, step):
        for copy in self.copies(part, step):
            copy.start()

    def finish(self, part, step):
        for copy in self.copies(part, step):
            copy.wait_recv()
        axis = PARTS[part][2][step]
        labels, source, rest = self.source(part, step)
        arrived = self.slots[part][2 * step]
        left = drop(labels, axis)
        for place in itertools.product(*[range(size) for size in sizes(left)]):
            where = dict(zip(left, place))
            where.update({k: self.c[k] for k in labels if k not in where})
            own = source[tuple(where[label] for label in labels) + rest].astype(F32)
            summed = own
            for slot in range(3):
                summed = summed + arrived[(slot,) + place].astype(F32)
            if step == 2:
                return summed
            self.slots[part][2 * step + 1][place] = summed.astype(BF)

    def drain(self):
        for part in range(3):
            for step in range(3):
                for copy in self.copies(part, step):
                    copy.wait_send()


def store_folded(part, summed, qkv_ref, proj_ref):
    start, stop, _ = PARTS[part]
    top, low = summed[:8], summed[8:]
    qkv_ref[:, start:stop] = top
    cut = min(max(1024 - start, 0), stop - start)
    if cut:
        qkv_ref[:, FOLD + start : FOLD + start + cut] = low[:, :cut]
    if cut < stop - start:
        proj_ref[:, start + cut - 1024 : stop - 1024] = low[:, cut:]


def block(at, size):
    return pl.ds(pl.multiple_of(at * size, size), size)


def loop(count, body, most=4):
    size = max(k for k in range(1, most + 1) if count % k == 0)

    def turn(at, carry):
        for k in range(size):
            body(at * size + k)
        return carry

    lax.fori_loop(0, count // size, turn, 0)


def dot(a, b):
    return jnp.dot(a, b, preferred_element_type=F32)


def dot_nt(a, b):
    return lax.dot_general(a, b, (((1,), (1,)), ((), ())), preferred_element_type=F32)


def dot_tn(a, b):
    return lax.dot_general(a, b, (((0,), (0,)), ((), ())), preferred_element_type=F32)


def normalised(x):
    centered = x - jnp.mean(x, axis=-1, keepdims=True)
    spread = jnp.mean(centered * centered, axis=-1, keepdims=True)
    scale = lax.rsqrt(spread + 1e-05)
    return centered * scale, scale


def norm_back(x, g):
    hat, scale = normalised(x)
    return scale * (
        g - jnp.mean(g, axis=-1, keepdims=True) - hat * jnp.mean(g * hat, axis=-1, keepdims=True)
    )


def by_head(pair, scale=1.0):
    lane = lax.broadcasted_iota(jnp.int32, (1, 128), 1)
    first = jnp.where(lane < 64, scale, 0.0).astype(BF)
    second = jnp.where(lane < 64, 0.0, scale).astype(BF)
    return jnp.concatenate([pair * first, pair * second], axis=0)


def side_by_side(stacked):
    return jnp.concatenate([stacked[:128], stacked[128:]], axis=1)


def attend(units, allowed):
    ones = by_head(jnp.ones((128, 128), BF))
    scores = [dot_nt(by_head(q, 0.125), k) for q, k, _ in units]
    if allowed is not None:
        scores = [
            jnp.where(allowed[None], one.reshape(2, 128, 128), -1e30).reshape(256, 128)
            for one in scores
        ]
    expo = [jnp.exp(one - jnp.max(one, axis=-1, keepdims=True)).astype(BF) for one in scores]
    found = []
    for one, (_, _, v) in zip(expo, units):
        both = dot(side_by_side(one), jnp.concatenate([by_head(v), ones], axis=1))
        over = 1.0 / both[:, 128:]
        found.append((one, over.astype(BF), (both[:, :128] * over).astype(BF)))
    return found


def attend_back(units):
    minus = jnp.full((128, 128), -1.0, BF)
    found = []
    for q, k, v, expo, over, mixed, g in units:
        g = g * over
        both = by_head(g)
        change = dot_nt(
            jnp.concatenate([both, by_head(g * mixed)], axis=1),
            jnp.concatenate([v, minus], axis=1),
        )
        grad_scores = (expo.astype(F32) * change).astype(BF)
        grad_q = dot(side_by_side(grad_scores), by_head(k, 0.125))
        grad_k = dot_tn(grad_scores, by_head(q, 0.125))
        grad_v = dot_tn(expo, both)
        found.append((grad_q.astype(BF), grad_k.astype(BF), grad_v.astype(BF)))
    return found


def pack_columns(rows):
    n = rows.shape[0] // 32
    width = rows.shape[1]
    late = rows.reshape(n, 2, 16, width)[:, :, 8:, :]
    place = lax.broadcasted_iota(jnp.int32, (n, 8, width), 1)
    both = jnp.where(place < 4, pltpu.roll(late[:, 0], 4, 1), late[:, 1])
    return both.reshape(n * 8, width).astype(BF)


def put_columns(rows, packed):
    n = rows.shape[0] // 32
    width = rows.shape[1]
    pairs = rows.reshape(n, 2, 16, width)
    arrived = packed.astype(F32).reshape(n, 8, width)
    place = lax.broadcasted_iota(jnp.int32, (n, 8, width), 1)
    even = jnp.where(place >= 4, pltpu.roll(arrived, 4, 1), pairs[:, 0, 8:])
    odd = jnp.where(place >= 4, arrived, pairs[:, 1, 8:])
    whole = jnp.concatenate([pairs[:, 0, :8], even, pairs[:, 1, :8], odd], axis=1)
    return whole.reshape(n * 32, width)


class Halo:

    def __init__(self, field, scratch, way, start=0):
        self.field, self.first = field, start
        self.packed, self.columns, self.rows, self.send_sem, self.recv_sem = scratch
        self.way = way

    def pack(self, half):
        def body(at):
            at = at + 4 * half
            rows = self.field[pl.ds(pl.multiple_of(at * 128 + self.first, 64), 128)]
            self.packed[block(at, 32)] = pack_columns(rows.astype(F32))

        loop(4, body)

    def copies(self):
        lat, lon = lax.axis_index("lat"), lax.axis_index("lon")
        way = self.way
        lat_to, lon_to = (lat + way) % LATS, (lon + way) % LONS
        if way == 1:
            plan = (
                (self.field.at[self.first + 960 : self.first + 1024], self.rows.at[:], (lat_to, lon)),
                (self.packed.at[240:256], self.columns.at[0:16], (lat_to, lon_to)),
                (self.packed.at[0:128], self.columns.at[16:144], (lat, lon_to)),
                (self.packed.at[128:240], self.columns.at[144:256], (lat, lon_to)),
            )
        else:
            plan = (
                (self.field.at[0:64], self.rows.at[:], (lat_to, lon)),
                (self.packed.at[0:16], self.columns.at[240:256], (lat_to, lon_to)),
                (self.packed.at[16:128], self.columns.at[0:112], (lat, lon_to)),
                (self.packed.at[128:256], self.columns.at[112:240], (lat, lon_to)),
            )
        return [
            remote(source, target, self.send_sem.at[k], self.recv_sem.at[k], device)
            for k, (source, target, device) in enumerate(plan)
        ]

    def start(self, which):
        copies = self.copies()
        for k in which:
            copies[k].start()

    def wait(self, which):
        copies = self.copies()
        for k in which:
            copies[k].wait_recv()

    def drain(self):
        for copy in self.copies():
            copy.wait_send()

    def assemble(self, part, write):
        if self.way == 1:
            if part == 0:
                write(0, put_columns(self.rows[...].astype(F32), self.columns[0:16]))

            def patch(at):
                at = at + 8 * part
                rows = self.field[pl.ds(pl.multiple_of(at * 64 + self.first, 64), 64)]
                write(at + 1, put_columns(rows.astype(F32), self.columns[block(at + 1, 16)]))

            loop(7 if part else 8, patch, 8)
        else:
            if part == 0:
                write(15, put_columns(self.rows[...].astype(F32), self.columns[240:256]))

            def patch(at):
                at = at + 7 * part
                rows = self.field[block(at + 1, 64)]
                write(at, put_columns(rows.astype(F32), self.columns[block(at, 16)]))

            loop(8 if part else 7, patch, 8)


def halo_scratch():
    return [
        pltpu.VMEM((256, C1), BF),
        pltpu.VMEM((256, C1), BF),
        pltpu.VMEM((64, C1), BF),
        pltpu.SemaphoreType.DMA((4,)),
        pltpu.SemaphoreType.DMA((4,)),
    ]


class Rows:

    def __init__(self, source, target, sems):
        self.source, self.target = source, target
        self.send_sem, self.recv_sem = sems

    def copy(self, by):
        lat, lon = lax.axis_index("lat"), lax.axis_index("lon")
        to = (lon + by) % LONS
        return remote(
            self.source.at[block(to, 16)],
            self.target.at[block(lon, 16)],
            self.send_sem.at[by],
            self.recv_sem.at[by],
            (lat, to),
        )

    def start(self):
        loop(15, lambda at: self.copy(at + 1).start(), 1)
        lon = lax.axis_index("lon")
        self.target[block(lon, 16)] = self.source[block(lon, 16)]

    def wait(self):
        loop(15, lambda at: self.copy(at + 1).wait_recv(), 1)

    def drain(self):
        loop(15, lambda at: self.copy(at + 1).wait_send(), 1)


def spread_lanes(ref, at, rows):
    for k in range(4):
        ref[k, block(at, 64)] = rows[:, 128 * k : 128 * k + 128]


def fine_pieces(ref, at):
    found = {}
    for b in range(2):
        lanes = [ref[k, pl.ds(at * 64 + b, 32, 2), :] for k in range(4)]
        rows = jnp.concatenate(lanes, axis=1).reshape(2, 2, 8, C1)
        for a in range(2):
            found[a, b] = rows[:, a].reshape(16, C1)
    return [found[a, b] for a in range(2) for b in range(2)]


def put_pieces(ref, at, pieces):
    for b in range(2):
        rows = jnp.stack(
            [pieces[b].reshape(2, 8, C1), pieces[2 + b].reshape(2, 8, C1)], axis=1
        ).reshape(32, C1)
        for k in range(4):
            ref[k, pl.ds(at * 64 + b, 32, 2), :] = rows[:, 128 * k : 128 * k + 128]


def joined_rows(ref, at, width):
    return jnp.concatenate([ref[k, block(at, 64)] for k in range(4)], axis=1)


def by_row(x, width):
    x = x.reshape(-1, 2, 8, width)
    return x[:, 0], x[:, 1]


WEIGHTS = dict(
    unmerge=(C2, 4 * C1),
    qkv_one=(C1, 3 * C1),
    proj_one=(C1, C1),
    merge=(4 * C1, C2),
    qkv_two=(C2, 3 * C2),
    proj_two=(C2, C2),
)

BUFFERS = dict(
    window=((TOKENS + 64, C1), BF),
    labels=((8, 128), F32),
    normed_one=((TOKENS, C1), BF),
    packed_one=((TOKENS, 3 * C1), BF),
    expo_one=((32, 256, 128), BF),
    over_one=((32, 128, 128), BF),
    mixed_one=((TOKENS, C1), BF),
    y_shift=((TOKENS, C1), BF),
    outgoing=((TOKENS, C1), BF),
    fine=((COARSE, 4 * C1), BF),
    spare=((4, TOKENS, 128), F32),
    grouped=((COARSE, 4 * C1), BF),
    coarse=((COARSE, C2), BF),
    coarse_rows=((COARSE, C2), BF),
    grad_skip_rows=((COARSE, C2), BF),
    normed_two=((COARSE, C2), BF),
    packed_two=((COARSE, 3 * C2), BF),
    expo_two=((16, 256, 128), BF),
    over_two=((16, 128, 128), BF),
    mixed_two=((COARSE, C2), BF),
    grad_mixed_two=((COARSE, C2), BF),
    wide=((COARSE, C2), F32),
    level_two_rows=((COARSE, C2), BF),
    level_two=((COARSE, C2), BF),
    grad_coarse_rows=((COARSE, C2), BF),
    grad_coarse=((COARSE, C2), BF),
    left_q=((512, 512), BF),
    left_p=((512, 512), BF),
    leave=((2, 512, 256), BF),
    right_q=((2 * COARSE, 3 * C2), BF),
    right_p=((2 * COARSE, C2), BF),
)


def scratch_list():
    shapes = [pltpu.VMEM(shape, BF) for shape in WEIGHTS.values()]
    shapes += [pltpu.VMEM(shape, dtype) for shape, dtype in BUFFERS.values()]
    shapes += [pltpu.SemaphoreType.DMA((len(WEIGHTS),)), pltpu.SemaphoreType.DMA((5,))]
    shapes += [pltpu.SemaphoreType.DMA((4,)), pltpu.SemaphoreType.DMA((4,))]
    shapes += [pltpu.SemaphoreType.DMA((LONS,)) for _ in range(8)]
    for _ in range(4):
        shapes += halo_scratch()
    return shapes + reduce_scratch()


def whole_kernel(*refs):
    region, tokens, cotangent = refs[:3]
    stored = refs[3:9]
    out_ref, grad_ref, qkv_ref, proj_ref = refs[9:13]
    scratch = list(refs[13:])

    def take(count):
        taken = scratch[:count]
        del scratch[:count]
        return taken

    weight = SimpleNamespace(**dict(zip(WEIGHTS, take(len(WEIGHTS)))))
    buf = SimpleNamespace(**dict(zip(BUFFERS, take(len(BUFFERS)))))
    load_sem, field_sem = take(2)
    pair_send, pair_recv = take(2)
    row_sems = [take(2) for _ in range(4)]
    halos = [take(5) for _ in range(4)]
    reducer = Reducer(take(len(reduce_scratch())))
    c = reducer.c
    lat, lon = lax.axis_index("lat"), lax.axis_index("lon")

    partners = [(lat, (lon + by) % LONS) for by in range(1, LONS)]
    for way in (1, -1):
        partners.append(((lat + way) % LATS, lon))
        partners.append(((lat + way) % LATS, (lon + way) % LONS))
    partners += [device_of(moved(c, axis, by)) for axis in ("x", "y", "z") for by in (1, 2, 3)]
    barrier = pltpu.get_barrier_semaphore()
    for partner in partners:
        pl.semaphore_signal(barrier, inc=1, device_id=partner, device_id_type=MESH)

    loads = {
        name: pltpu.make_async_copy(source, getattr(weight, name), load_sem.at[k])
        for k, (name, source) in enumerate(zip(WEIGHTS, stored))
    }
    token_load = pltpu.make_async_copy(tokens, buf.window.at[64:1088], field_sem.at[0])
    cotangent_load = pltpu.make_async_copy(cotangent, buf.mixed_one, field_sem.at[1])
    cotangent_again = pltpu.make_async_copy(cotangent, buf.y_shift, field_sem.at[2])
    output_store = pltpu.make_async_copy(buf.outgoing, out_ref, field_sem.at[3])
    grad_store = pltpu.make_async_copy(buf.outgoing, grad_ref, field_sem.at[4])
    token_load.start()
    cotangent_load.start()
    for copy in loads.values():
        copy.start()
    loads = SimpleNamespace(**loads)

    column = lax.broadcasted_iota(jnp.int32, (16, 128), 0)
    place = lax.broadcasted_iota(jnp.int32, (16, 128), 1) & 15
    chosen = jnp.where(column == ((place + 4) & 15), 1.0, 0.0).astype(BF)
    spread_region = dot_tn(region[...].astype(F32).astype(BF), chosen).reshape(8, 8, 128)
    row = lax.broadcasted_iota(jnp.int32, (8, 8, 128), 1)
    token = lax.broadcasted_iota(jnp.int32, (8, 8, 128), 2)
    own_row = jnp.where(row == (token >> 4), spread_region, 0.0)
    second = jnp.where(((token + 4) & 15) >= 8, 1.0, 0.0)[:, 0]
    buf.labels[...] = jnp.sum(own_row, axis=1) * 2.0 + second

    tokens_in = Halo(buf.window, halos[0], 1, 64)
    fine_back = Halo(buf.y_shift, halos[1], -1)
    grads_in = Halo(buf.normed_one, halos[2], 1)
    grads_back = Halo(buf.y_shift, halos[3], -1)
    skip_to_rows = Rows(buf.grad_mixed_two, buf.grad_skip_rows, row_sems[0])
    coarse_to_rows = Rows(buf.coarse, buf.coarse_rows, row_sems[1])
    level_to_tile = Rows(buf.level_two_rows, buf.level_two, row_sems[2])
    grad_to_tile = Rows(buf.grad_coarse_rows, buf.grad_coarse, row_sems[3])

    with jax.named_scope("tokens_in"):
        token_load.wait()
        tokens_in.pack(0)
        tokens_in.pack(1)
        pl.semaphore_wait(barrier, len(partners))
        tokens_in.start(range(4))

    with jax.named_scope("grad_skip"):
        cotangent_load.wait()

        def spread(at):
            spread_lanes(buf.spare, at, buf.mixed_one[block(at, 64)].astype(F32))

        loop(16, spread)

        def group_cotangent(at):
            buf.grouped[block(at, 16)] = jnp.concatenate(
                fine_pieces(buf.spare, at), axis=1
            ).astype(BF)

        loop(16, group_cotangent)

    def lanes(third, pair):
        return slice(C1 * third + 128 * pair, C1 * third + 128 * pair + 128)

    def windows_allowed(group):
        row = jnp.broadcast_to(buf.labels[pl.ds(group, 1), :], (128, 128))
        return row == row.T

    with jax.named_scope("level_one"):
        def write_window(at, rows):
            buf.window[block(at, 64)] = rows.astype(BF)
            buf.normed_one[block(at, 64)] = normalised(rows)[0].astype(BF)

        loads.qkv_one.wait()
        loads.proj_one.wait()
        for half in range(2):
            tokens_in.wait((3,) if half else (0, 1, 2))
            tokens_in.assemble(half, write_window)
            rows = slice(512 * half, 512 * half + 512)

            def project(at):
                buf.packed_one[rows, block(at, 256)] = dot(
                    buf.normed_one[rows], weight.qkv_one[:, block(at, 256)]
                ).astype(BF)

            loop(6, project, DENSE)

            def attend_group(at):
                group = at + 4 * half
                where = block(group, 128)
                units = [
                    [buf.packed_one[where, lanes(third, pair)] for third in range(3)]
                    for pair in range(4)
                ]
                for pair, found in enumerate(attend(units, windows_allowed(group))):
                    at_unit = group * 4 + pair
                    buf.expo_one[at_unit], buf.over_one[at_unit], mixed = found
                    buf.mixed_one[where, lanes(0, pair)] = mixed

            loop(4, attend_group, HEADS)

            def add_tokens(at):
                columns = block(at, 256)
                buf.y_shift[rows, columns] = (
                    buf.window[rows, columns].astype(F32)
                    + dot(buf.mixed_one[rows], weight.proj_one[:, columns])
                ).astype(BF)

            loop(2, add_tokens, DENSE)
            fine_back.pack(half)
            fine_back.start((0, 1, 2) if half == 0 else (3,))

    with jax.named_scope("merge"):
        loads.unmerge.wait()

        def grad_skip(at):
            buf.grad_mixed_two[:, block(at, 256)] = dot_nt(
                buf.grouped[...], weight.unmerge[block(at, 256)]
            ).astype(BF)

        loop(4, grad_skip, DENSE)
        skip_to_rows.start()

        def write_fine(at, rows):
            spread_lanes(buf.spare, at, rows.astype(BF).astype(F32))

        fine_back.wait((0, 1, 2))
        fine_back.assemble(0, write_fine)
        fine_back.wait((3,))
        fine_back.assemble(1, write_fine)

        def group_fine(at):
            whole = jnp.concatenate(fine_pieces(buf.spare, at), axis=1)
            buf.fine[block(at, 16)] = whole.astype(BF)
            buf.grouped[block(at, 16)] = normalised(whole)[0].astype(BF)

        loop(16, group_fine)
        loads.merge.wait()

        def merge(at):
            columns = block(at, 256)
            buf.coarse[:, columns] = dot(
                buf.grouped[...], weight.merge[:, columns]
            ).astype(BF)

        loop(4, merge, DENSE)
        coarse_to_rows.start()
        fine_back.drain()
        cotangent_again.start()

    with jax.named_scope("level_two"):
        loads.qkv_two.wait()
        loads.proj_two.wait()
        coarse_to_rows.wait()

        def norm_two(at):
            both = by_row(buf.coarse_rows[block(at, 64)].astype(F32), C2)
            for row in range(2):
                x = both[row].reshape(32, C2)
                where = pl.ds(pl.multiple_of(at * 32 + 128 * row, 32), 32)
                buf.wide[where] = x
                buf.normed_two[where] = normalised(x)[0].astype(BF)

        loop(4, norm_two)

        def project_two(at):
            columns = block(at, 256)
            buf.packed_two[:, columns] = dot(
                buf.normed_two[...], weight.qkv_two[:, columns]
            ).astype(BF)

        loop(12, project_two, DENSE)

        def operands_two(row, pair):
            rows = slice(128 * row, 128 * row + 128)
            return [
                buf.packed_two[rows, pl.ds(pl.multiple_of(C2 * third + pair * 128, 128), 128)]
                for third in range(3)
            ]

        def attend_two(at):
            places = [(2 * at + k, row) for k in range(2) for row in range(2)]
            units = [operands_two(row, pair) for pair, row in places]
            for (pair, row), found in zip(places, attend(units, None)):
                at_unit = pair * 2 + row
                buf.expo_two[at_unit], buf.over_two[at_unit], mixed = found
                buf.mixed_two[128 * row : 128 * row + 128, block(pair, 128)] = mixed

        loop(4, attend_two, HEADS)

        def add_coarse(at):
            columns = block(at, 256)
            total = buf.wide[:, columns] + dot(buf.mixed_two[...], weight.proj_two[:, columns])
            buf.level_two_rows[:, columns] = (
                jnp.stack([total[:128].reshape(16, 8, 256), total[128:].reshape(16, 8, 256)], axis=1)
                .reshape(256, 256)
                .astype(BF)
            )

        loop(4, add_coarse, DENSE)
        level_to_tile.start()

    with jax.named_scope("grad_level_two"):
        skip_to_rows.wait()

        def grad_level(at):
            x = buf.level_two_rows[block(at, 64)].astype(F32)
            g = buf.grad_skip_rows[block(at, 64)].astype(F32)
            both = by_row(norm_back(x, g), C2)
            for row in range(2):
                where = pl.ds(pl.multiple_of(at * 32 + 128 * row, 32), 32)
                buf.right_p[where] = both[row].reshape(32, C2).astype(BF)

        loop(4, grad_level)
        skip_to_rows.drain()

        def grad_mixed(at):
            buf.grad_mixed_two[:, block(at, 256)] = dot_nt(
                buf.right_p[0:256], weight.proj_two[block(at, 256)]
            ).astype(BF)

        loop(4, grad_mixed, DENSE)

        def attend_two_back(at):
            places = [(2 * at + k, row) for k in range(2) for row in range(2)]
            units = []
            for pair, row in places:
                rows = slice(128 * row, 128 * row + 128)
                units.append(
                    operands_two(row, pair)
                    + [
                        buf.expo_two[pair * 2 + row],
                        buf.over_two[pair * 2 + row],
                        buf.mixed_two[rows, block(pair, 128)],
                        buf.grad_mixed_two[rows, block(pair, 128)],
                    ]
                )
            for (pair, row), found in zip(places, attend_back(units)):
                for third in range(3):
                    where = pl.ds(pl.multiple_of(C2 * third + pair * 128, 128), 128)
                    buf.right_q[128 * row : 128 * row + 128, where] = found[third]

        loop(4, attend_two_back, HEADS)

    def turn(source, left, slot):
        first = c["core"] == 0
        for half in range(2):
            tokens_at = slice(128 * half, 128 * half + 128)
            groups = source[tokens_at].astype(F32).T.reshape(64, 2, 8, 128)
            mine = jnp.where(first, groups[:, 0], groups[:, 1])
            theirs = jnp.where(first, groups[:, 1], groups[:, 0])
            left[:, tokens_at] = mine.reshape(512, 128).astype(BF)
            buf.leave[slot, :, tokens_at] = theirs.reshape(512, 128).astype(BF)

    pair_copies = [
        remote(source, target, pair_send.at[k], pair_recv.at[k], device_of(moved(c, "core", 1)))
        for k, (source, target) in enumerate(
            (
                (buf.right_q.at[0:256], buf.right_q.at[256:512]),
                (buf.right_p.at[0:256], buf.right_p.at[256:512]),
                (buf.leave.at[0], buf.left_q.at[:, 256:512]),
                (buf.leave.at[1], buf.left_p.at[:, 256:512]),
            )
        )
    ]

    with jax.named_scope("grad_coarse"):
        pair_copies[0].start()
        pair_copies[1].start()

        def grad_normed_two(at):
            buf.grad_mixed_two[:, block(at, 256)] = dot_nt(
                buf.right_q[0:256], weight.qkv_two[block(at, 256)]
            ).astype(BF)

        loop(4, grad_normed_two, DENSE)

        def grad_coarse(at):
            both = []
            for row in range(2):
                where = pl.ds(pl.multiple_of(at * 32 + 128 * row, 32), 32)
                g = norm_back(buf.wide[where], buf.grad_mixed_two[where].astype(F32))
                g = g.astype(BF).astype(F32) + buf.right_p[where].astype(F32)
                both.append(g.reshape(4, 8, C2))
            buf.grad_coarse_rows[block(at, 64)] = (
                jnp.stack(both, axis=1).reshape(64, C2).astype(BF)
            )

        loop(4, grad_coarse)
        grad_to_tile.start()

    with jax.named_scope("weight_gradients"):
        turn(buf.normed_two, buf.left_q, 0)
        pair_copies[2].start()
        turn(buf.mixed_two, buf.left_p, 1)
        pair_copies[3].start()
        for copy in pair_copies:
            copy.wait_recv()

        def put_total(zh, columns, top, low):
            width = top.shape[1]
            both = jnp.concatenate([top.reshape(32, 8, width), low.reshape(32, 8, width)], axis=1)
            reducer.total[zh, :, :, :, :, columns] = both.astype(BF).reshape(4, 2, 4, 16, width)

        def narrow_tile(at):
            right = jnp.concatenate(
                [buf.right_q[:, block(at, 128)], buf.right_q[:, block(at + 16, 128)]], axis=1
            )
            for zh in range(2):
                both = dot(buf.left_q[256 * zh : 256 * zh + 256], right)
                put_total(zh, block(at, 128), both[:, :128], both[:, 128:])

        def wide_tile(at):
            for zh in range(2):
                rows = slice(256 * zh, 256 * zh + 256)
                top = dot(buf.left_q[rows], buf.right_q[:, block(at, 256)])
                low = dot(buf.left_p[rows], buf.right_p[:, block(at - 4, 256)])
                put_total(zh, block(at, 256), top, low)

        for part, (start, stop, _) in enumerate(PARTS):
            middle = max(start, min(stop, 1024))
            if middle > start:
                loop((middle - start) // 128, lambda at: narrow_tile(at + start // 128), TILES)
            if stop > middle:
                loop((stop - middle) // 256, lambda at: wide_tile(at + middle // 256), TILES)
            reducer.start(part, 0)

    with jax.named_scope("grad_fine"):
        grad_to_tile.wait()

        def grad_grouped(at):
            buf.grouped[:, block(at, 256)] = dot_nt(
                buf.grad_coarse[...], weight.merge[block(at, 256)]
            ).astype(BF)

        loop(8, grad_grouped, DENSE)

        def grad_pieces(at):
            g = norm_back(
                buf.fine[block(at, 16)].astype(F32), buf.grouped[block(at, 16)].astype(F32)
            )
            put_pieces(buf.spare, at, [g[:, C1 * k : C1 * k + C1] for k in range(4)])

        loop(16, grad_pieces)

        cotangent_again.wait()

        def grad_fine(at):
            buf.normed_one[block(at, 64)] = (
                joined_rows(buf.spare, at, C1) + buf.y_shift[block(at, 64)].astype(F32)
            ).astype(BF)

        loop(16, grad_fine)
        grads_in.pack(0)
        grads_in.pack(1)
        grads_in.start(range(4))

    with jax.named_scope("output"):
        level_to_tile.wait()

        def norm_level(at):
            x = buf.level_two[block(at, 64)].astype(F32)
            buf.coarse[block(at, 64)] = normalised(x)[0].astype(BF)

        coarse_to_rows.drain()
        loop(4, norm_level)

        for half in range(2):
            rows = slice(128 * half, 128 * half + 128)

            def unmerge(at):
                for low in range(2):
                    buf.wide[128 * low : 128 * low + 128, block(at, 256)] = dot(
                        buf.coarse[rows], weight.unmerge[:, block(at + 4 * low, 256)]
                    )

            loop(4, unmerge, DENSE)

            def add_fine(at):
                fine = buf.fine[block(at + 8 * half, 16)].astype(F32)
                upper = jnp.concatenate(
                    [buf.wide[block(at, 16)], buf.wide[block(at + 8, 16)]], axis=1
                )
                total = fine + upper
                put_pieces(
                    buf.spare,
                    at + 8 * half,
                    [total[:, C1 * k : C1 * k + C1] for k in range(4)],
                )

            loop(8, add_fine)

        def write_output(at):
            buf.outgoing[block(at, 64)] = joined_rows(buf.spare, at, C1).astype(BF)

        loop(16, write_output)
        output_store.start()

    with jax.named_scope("grad_level_one"):

        def write_grads(at, rows):
            buf.y_shift[block(at, 64)] = rows.astype(BF)

        grads_in.wait(range(4))
        grads_in.assemble(0, write_grads)
        grads_in.assemble(1, write_grads)
        grads_in.drain()
        for half in range(2):
            rows = slice(512 * half, 512 * half + 512)

            def grad_mixed_one(at):
                buf.normed_one[rows, block(at, 256)] = dot_nt(
                    buf.y_shift[rows], weight.proj_one[block(at, 256)]
                ).astype(BF)

            loop(2, grad_mixed_one, DENSE)

            def attend_group_back(at):
                group = at + 4 * half
                where = block(group, 128)
                units = []
                for pair in range(4):
                    at_unit = group * 4 + pair
                    units.append(
                        [buf.packed_one[where, lanes(third, pair)] for third in range(3)]
                        + [
                            buf.expo_one[at_unit],
                            buf.over_one[at_unit],
                            buf.mixed_one[where, lanes(0, pair)],
                            buf.normed_one[where, lanes(0, pair)],
                        ]
                    )
                for pair, found in enumerate(attend_back(units)):
                    for third in range(3):
                        buf.packed_one[where, lanes(third, pair)] = found[third]

            loop(4, attend_group_back, HEADS)

            def grad_normed_one(at):
                buf.normed_one[rows, block(at, 256)] = dot_nt(
                    buf.packed_one[rows], weight.qkv_one[block(at, 256)]
                ).astype(BF)

            loop(2, grad_normed_one, DENSE)

            def grad_window(at):
                where = block(at + 8 * half, 64)
                g = norm_back(
                    buf.window[where].astype(F32), buf.normed_one[where].astype(F32)
                )
                buf.y_shift[where] = (g + buf.y_shift[where].astype(F32)).astype(BF)

            loop(8, grad_window)
            grads_back.pack(half)
            grads_back.start((0, 1, 2) if half == 0 else (3,))
            for part in range(3):
                reducer.finish(part, half)
                reducer.start(part, half + 1)

    with jax.named_scope("grad_tokens"):
        output_store.wait()

        def write_tokens(at, rows):
            buf.outgoing[block(at, 64)] = rows.astype(BF)

        grads_back.wait((0, 1, 2))
        grads_back.assemble(0, write_tokens)
        grads_back.wait((3,))
        grads_back.assemble(1, write_tokens)
        grad_store.start()
        for part in range(3):
            store_folded(part, reducer.finish(part, 2), qkv_ref, proj_ref)

    tokens_in.drain()
    grads_back.drain()
    level_to_tile.drain()
    grad_to_tile.drain()
    for copy in pair_copies:
        copy.wait_send()
    reducer.drain()
    grad_store.wait()


def hand_over(*refs):
    for source, target in zip(refs[:4], refs[4:]):
        target[...] = source[...]


def body(
    tokens, region, qkv_one, proj_one, merge_weight, qkv_two, proj_two, unmerge_weight, cotangent
):
    vmem = pl.BlockSpec(memory_space=pltpu.VMEM)
    anywhere = pl.BlockSpec(memory_space=pl.ANY)
    shapes = (
            jax.ShapeDtypeStruct((TOKENS, C1), BF),
            jax.ShapeDtypeStruct((TOKENS, C1), BF),
            jax.ShapeDtypeStruct((8, 3 * C2), F32),
            jax.ShapeDtypeStruct((8, C2), F32),
    )
    found = pl.pallas_call(
        whole_kernel,
        out_shape=shapes,
        in_specs=[vmem] + [anywhere] * 8,
        out_specs=(anywhere, anywhere, vmem, vmem),
        scratch_shapes=scratch_list(),
        compiler_params=pltpu.CompilerParams(
            collective_id=0, has_side_effects=True, vmem_limit_bytes=VMEM_LIMIT
        ),
    )(
        region.T,
        tokens.reshape(TOKENS, C1),
        cotangent.reshape(TOKENS, C1),
        unmerge_weight,
        qkv_one,
        proj_one,
        merge_weight,
        qkv_two,
        proj_two,
    )
    pieces = [
        pl.BlockSpec((TOKENS // 4, C1), lambda at: (at, 0)),
        pl.BlockSpec((TOKENS // 4, C1), lambda at: (at, 0)),
        pl.BlockSpec((8, 3 * C2 // 4), lambda at: (0, at)),
        pl.BlockSpec((8, C2 // 4), lambda at: (0, at)),
    ]
    output, grad_tokens, grad_qkv_two, grad_proj_two = pl.pallas_call(
        hand_over, grid=(4,), out_shape=shapes, in_specs=pieces, out_specs=pieces
    )(*found)
    shape = tokens.shape
    return output.reshape(shape), grad_tokens.reshape(shape), grad_qkv_two, grad_proj_two


def solution(mesh):
    return jax.shard_map(
        body,
        mesh=mesh,
        in_specs=(
            P("lat", "lon", None),
            P("lat", "lon"),
            P(),
            P(),
            P(),
            P(),
            P(),
            P(),
            P("lat", "lon", None),
        ),
        out_specs=(
            P("lat", "lon", None),
            P("lat", "lon", None),
            P(("lat", "lon"), None),
            P(("lat", "lon"), None),
        ),
        check_vma=False,
    )
```

```python
import itertools
from types import SimpleNamespace

import jax
import jax.numpy as jnp
from jax import lax
from jax.experimental import pallas as pl
from jax.experimental.pallas import tpu as pltpu
from jax.sharding import PartitionSpec as P

MESH = pl.DeviceIdType.MESH
BF = jnp.bfloat16
F32 = jnp.float32
VMEM_LIMIT = 63 * 1024 * 1024

TOKENS, C1, C2 = 1024, 512, 1024
COARSE = 256
LONS, LATS = 16, 8
DENSE, HEADS, TILES = 4, 1, 1

FOLD = 2048
PARTS = ((0, 640, ("x", "y", "z")), (640, 1280, ("y", "z", "x")), (1280, 2048, ("z", "x", "y")))
LABELS = ("zh", "x", "zl", "y")


def coordinates():
    lat, lon = lax.axis_index("lat"), lax.axis_index("lon")
    return {
        "zh": lat // 4,
        "x": lat % 4,
        "zl": lon // 8,
        "y": (lon // 2) % 4,
        "core": lon % 2,
    }


def device_of(c):
    return (c["zh"] * 4 + c["x"], (c["zl"] * 4 + c["y"]) * 2 + c["core"])


def moved(c, axis, by):
    c = dict(c)
    if axis == "z":
        z = (c["zh"] * 2 + c["zl"] + by) % 4
        c["zh"], c["zl"] = z // 2, z % 2
    elif axis == "core":
        c["core"] = 1 - c["core"]
    else:
        c[axis] = (c[axis] + by) % 4
    return c


def pick(labels, axis, c):
    names = ("zh", "zl") if axis == "z" else (axis,)
    return tuple(c[label] if label in names else slice(None) for label in labels)


def drop(labels, axis):
    names = ("zh", "zl") if axis == "z" else (axis,)
    return tuple(label for label in labels if label not in names)


def sizes(labels):
    return tuple(4 if label in ("x", "y") else 2 for label in labels)


def remote(source, target, send_sem, recv_sem, device):
    return pltpu.make_async_remote_copy(
        src_ref=source,
        dst_ref=target,
        send_sem=send_sem,
        recv_sem=recv_sem,
        device_id=device,
        device_id_type=MESH,
    )


def reduce_scratch():
    shapes = [pltpu.VMEM((2, 4, 2, 4, 16, FOLD), BF)]
    for start, stop, order in PARTS:
        labels = LABELS
        for step, axis in enumerate(order):
            labels = drop(labels, axis)
            shapes.append(pltpu.VMEM((3,) + sizes(labels) + (16, stop - start), BF))
            if step < 2:
                shapes.append(pltpu.VMEM(sizes(labels) + (16, stop - start), BF))
    shapes += [pltpu.SemaphoreType.DMA((3, 3, 3)), pltpu.SemaphoreType.DMA((3, 3, 3))]
    return shapes + [pltpu.SemaphoreType.DMA((3, 6)), pltpu.SemaphoreType.DMA((3, 6))]


class Reducer:
    def __init__(self, scratch):
        self.total = scratch[0]
        self.slots = [scratch[1 + 5 * p : 6 + 5 * p] for p in range(3)]
        self.send_sem, self.recv_sem, self.ring_send, self.ring_recv = scratch[16:]
        self.c = coordinates()

    def source(self, part, step):
        start, stop, order = PARTS[part]
        labels = LABELS
        for axis in order[:step]:
            labels = drop(labels, axis)
        if step == 0:
            return labels, self.total, (slice(None), pl.ds(start, stop - start))
        return labels, self.slots[part][2 * step - 1], (slice(None), slice(None))

    def copies(self, part, step):
        axis = PARTS[part][2][step]
        labels, source, rest = self.source(part, step)
        found = []
        for by in (2, 1, 3):
            target = moved(self.c, axis, by)
            found.append(
                remote(
                    source.at[pick(labels, axis, target) + rest],
                    self.slots[part][2 * step].at[by - 1],
                    self.send_sem.at[part, step, by - 1],
                    self.recv_sem.at[part, step, by - 1],
                    device_of(target),
                )
            )
        return found

    def ring(self, part):
        start, stop, order = PARTS[part]
        axis, width = order[0], stop - start
        cut = width // 256 * 128
        halves = ((0, cut), (cut, width - cut))
        after, before, opposite = (moved(self.c, axis, by) for by in (1, 3, 2))
        every = (slice(None),) * len(drop(LABELS, axis))

        def mine(owner, half):
            at, size = halves[half]
            return self.total.at[pick(LABELS, axis, owner) + (slice(None), pl.ds(start + at, size))]

        def slot(which, half):
            at, size = halves[half]
            return self.slots[part][0].at[(which,) + every + (slice(None), pl.ds(at, size))]

        plan = (
            (mine(opposite, 0), slot(2, 0), after),
            (mine(opposite, 1), slot(2, 1), before),
            (mine(after, 1), slot(0, 1), after),
            (mine(before, 0), slot(1, 0), before),
            (slot(2, 0), slot(0, 0), after),
            (slot(2, 1), slot(1, 1), before),
        )
        copies = [
            remote(source, target, self.ring_send.at[part, k], self.ring_recv.at[part, k], device_of(device))
            for k, (source, target, device) in enumerate(plan)
        ]
        return copies, halves, (after, before)

    def start(self, part, step):
        copies = self.copies(part, step) if step else self.ring(part)[0][:4]
        for copy in copies:
            copy.start()

    def pass_on(self, part):
        copies, halves, owners = self.ring(part)
        start, _, order = PARTS[part]
        left = drop(LABELS, order[0])
        passed = self.slots[part][0]
        for half, (at, size) in enumerate(halves):
            copies[half].wait_recv()
            for place in itertools.product(*[range(count) for count in sizes(left)]):
                where = {**owners[half], **dict(zip(left, place))}
                own = self.total[
                    tuple(where[label] for label in LABELS) + (slice(None), slice(start + at, start + at + size))
                ]
                here = (2,) + place + (slice(None), slice(at, at + size))
                passed[here] = (passed[here].astype(F32) + own.astype(F32)).astype(BF)
            copies[4 + half].start()

    def finish(self, part, step):
        copies = self.copies(part, step) if step else self.ring(part)[0][2:]
        for copy in copies:
            copy.wait_recv()
        axis = PARTS[part][2][step]
        labels, source, rest = self.source(part, step)
        arrived = self.slots[part][2 * step]
        left = drop(labels, axis)
        for place in itertools.product(*[range(size) for size in sizes(left)]):
            where = dict(zip(left, place))
            where.update({k: self.c[k] for k in labels if k not in where})
            own = source[tuple(where[label] for label in labels) + rest].astype(F32)
            summed = own
            for slot in range(3 if step else 2):
                summed = summed + arrived[(slot,) + place].astype(F32)
            if step == 2:
                return summed
            self.slots[part][2 * step + 1][place] = summed.astype(BF)

    def drain(self):
        for part in range(3):
            for copy in self.ring(part)[0]:
                copy.wait_send()
            for step in range(1, 3):
                for copy in self.copies(part, step):
                    copy.wait_send()


def store_folded(part, summed, qkv_ref, proj_ref):
    start, stop, _ = PARTS[part]
    top, low = summed[:8], summed[8:]
    qkv_ref[:, start:stop] = top
    cut = min(max(1024 - start, 0), stop - start)
    if cut:
        qkv_ref[:, FOLD + start : FOLD + start + cut] = low[:, :cut]
    if cut < stop - start:
        proj_ref[:, start + cut - 1024 : stop - 1024] = low[:, cut:]


def block(at, size):
    return pl.ds(pl.multiple_of(at * size, size), size)


def loop(count, body, most=4):
    size = max(k for k in range(1, most + 1) if count % k == 0)

    def turn(at, carry):
        for k in range(size):
            body(at * size + k)
        return carry

    lax.fori_loop(0, count // size, turn, 0)


def dot(a, b):
    return jnp.dot(a, b, preferred_element_type=F32)


def dot_nt(a, b):
    return lax.dot_general(a, b, (((1,), (1,)), ((), ())), preferred_element_type=F32)


def dot_tn(a, b):
    return lax.dot_general(a, b, (((0,), (0,)), ((), ())), preferred_element_type=F32)


def normalised(x):
    centered = x - jnp.mean(x, axis=-1, keepdims=True)
    spread = jnp.mean(centered * centered, axis=-1, keepdims=True)
    scale = lax.rsqrt(spread + 1e-05)
    return centered * scale, scale


def norm_back(x, g):
    hat, scale = normalised(x)
    return scale * (
        g - jnp.mean(g, axis=-1, keepdims=True) - hat * jnp.mean(g * hat, axis=-1, keepdims=True)
    )


def by_head(pair, scale=1.0):
    lane = lax.broadcasted_iota(jnp.int32, (1, 128), 1)
    first = jnp.where(lane < 64, scale, 0.0).astype(BF)
    second = jnp.where(lane < 64, 0.0, scale).astype(BF)
    return jnp.concatenate([pair * first, pair * second], axis=0)


def side_by_side(stacked):
    return jnp.concatenate([stacked[:128], stacked[128:]], axis=1)


def attend(units, allowed):
    ones = by_head(jnp.ones((128, 128), BF))
    scores = [dot_nt(by_head(q, 0.125), k) for q, k, _ in units]
    if allowed is not None:
        scores = [
            jnp.where(allowed[None], one.reshape(2, 128, 128), -1e30).reshape(256, 128)
            for one in scores
        ]
    expo = [jnp.exp(one - jnp.max(one, axis=-1, keepdims=True)).astype(BF) for one in scores]
    found = []
    for one, (_, _, v) in zip(expo, units):
        both = dot(side_by_side(one), jnp.concatenate([by_head(v), ones], axis=1))
        over = 1.0 / both[:, 128:]
        found.append((one, over.astype(BF), (both[:, :128] * over).astype(BF)))
    return found


def attend_back(units):
    minus = jnp.full((128, 128), -1.0, BF)
    found = []
    for q, k, v, expo, over, mixed, g in units:
        g = g * over
        both = by_head(g)
        change = dot_nt(
            jnp.concatenate([both, by_head(g * mixed)], axis=1),
            jnp.concatenate([v, minus], axis=1),
        )
        grad_scores = (expo.astype(F32) * change).astype(BF)
        grad_q = dot(side_by_side(grad_scores), by_head(k, 0.125))
        grad_k = dot_tn(grad_scores, by_head(q, 0.125))
        grad_v = dot_tn(expo, both)
        found.append((grad_q.astype(BF), grad_k.astype(BF), grad_v.astype(BF)))
    return found


def pack_columns(rows):
    n = rows.shape[0] // 32
    width = rows.shape[1]
    late = rows.reshape(n, 2, 16, width)[:, :, 8:, :]
    place = lax.broadcasted_iota(jnp.int32, (n, 8, width), 1)
    both = jnp.where(place < 4, pltpu.roll(late[:, 0], 4, 1), late[:, 1])
    return both.reshape(n * 8, width).astype(BF)


def put_columns(rows, packed):
    n = rows.shape[0] // 32
    width = rows.shape[1]
    pairs = rows.reshape(n, 2, 16, width)
    arrived = packed.astype(F32).reshape(n, 8, width)
    place = lax.broadcasted_iota(jnp.int32, (n, 8, width), 1)
    even = jnp.where(place >= 4, pltpu.roll(arrived, 4, 1), pairs[:, 0, 8:])
    odd = jnp.where(place >= 4, arrived, pairs[:, 1, 8:])
    whole = jnp.concatenate([pairs[:, 0, :8], even, pairs[:, 1, :8], odd], axis=1)
    return whole.reshape(n * 32, width)


class Halo:

    def __init__(self, field, scratch, way, start=0):
        self.field, self.first = field, start
        self.packed, self.columns, self.rows, self.send_sem, self.recv_sem = scratch
        self.way = way

    def pack(self, half):
        def body(at):
            at = at + 4 * half
            rows = self.field[pl.ds(pl.multiple_of(at * 128 + self.first, 64), 128)]
            self.packed[block(at, 32)] = pack_columns(rows.astype(F32))

        loop(4, body)

    def copies(self):
        lat, lon = lax.axis_index("lat"), lax.axis_index("lon")
        way = self.way
        lat_to, lon_to = (lat + way) % LATS, (lon + way) % LONS
        if way == 1:
            plan = (
                (self.field.at[self.first + 960 : self.first + 1024], self.rows.at[:], (lat_to, lon)),
                (self.packed.at[240:256], self.columns.at[0:16], (lat_to, lon_to)),
                (self.packed.at[0:128], self.columns.at[16:144], (lat, lon_to)),
                (self.packed.at[128:240], self.columns.at[144:256], (lat, lon_to)),
            )
        else:
            plan = (
                (self.field.at[0:64], self.rows.at[:], (lat_to, lon)),
                (self.packed.at[0:16], self.columns.at[240:256], (lat_to, lon_to)),
                (self.packed.at[16:128], self.columns.at[0:112], (lat, lon_to)),
                (self.packed.at[128:256], self.columns.at[112:240], (lat, lon_to)),
            )
        return [
            remote(source, target, self.send_sem.at[k], self.recv_sem.at[k], device)
            for k, (source, target, device) in enumerate(plan)
        ]

    def start(self, which):
        copies = self.copies()
        for k in which:
            copies[k].start()

    def wait(self, which):
        copies = self.copies()
        for k in which:
            copies[k].wait_recv()

    def drain(self):
        for copy in self.copies():
            copy.wait_send()

    def assemble(self, part, write):
        if self.way == 1:
            if part == 0:
                write(0, put_columns(self.rows[...].astype(F32), self.columns[0:16]))

            def patch(at):
                at = at + 8 * part
                rows = self.field[pl.ds(pl.multiple_of(at * 64 + self.first, 64), 64)]
                write(at + 1, put_columns(rows.astype(F32), self.columns[block(at + 1, 16)]))

            loop(7 if part else 8, patch, 8)
        else:
            if part == 0:
                write(15, put_columns(self.rows[...].astype(F32), self.columns[240:256]))

            def patch(at):
                at = at + 7 * part
                rows = self.field[block(at + 1, 64)]
                write(at, put_columns(rows.astype(F32), self.columns[block(at, 16)]))

            loop(8 if part else 7, patch, 8)


def halo_scratch():
    return [
        pltpu.VMEM((256, C1), BF),
        pltpu.VMEM((256, C1), BF),
        pltpu.VMEM((64, C1), BF),
        pltpu.SemaphoreType.DMA((4,)),
        pltpu.SemaphoreType.DMA((4,)),
    ]


class Rows:

    def __init__(self, source, target, sems):
        self.source, self.target = source, target
        self.send_sem, self.recv_sem = sems

    def copy(self, by):
        lat, lon = lax.axis_index("lat"), lax.axis_index("lon")
        to = (lon + by) % LONS
        return remote(
            self.source.at[block(to, 16)],
            self.target.at[block(lon, 16)],
            self.send_sem.at[by],
            self.recv_sem.at[by],
            (lat, to),
        )

    def start_to(self, to):
        lon = lax.axis_index("lon")
        by = (to - lon + LONS) % LONS

        @pl.when(by != 0)
        def _():
            self.copy(by).start()

        @pl.when(by == 0)
        def _():
            self.target[block(lon, 16)] = self.source[block(lon, 16)]

    def start(self, half):
        loop(8, lambda at: self.start_to(at + 8 * half), 1)

    def wait(self):
        loop(15, lambda at: self.copy(at + 1).wait_recv(), 1)

    def drain(self):
        loop(15, lambda at: self.copy(at + 1).wait_send(), 1)


def spread_lanes(ref, at, rows):
    for k in range(4):
        ref[k, block(at, 64)] = rows[:, 128 * k : 128 * k + 128]


def fine_pieces(ref, at):
    found = {}
    for b in range(2):
        lanes = [ref[k, pl.ds(at * 64 + b, 32, 2), :] for k in range(4)]
        rows = jnp.concatenate(lanes, axis=1).reshape(2, 2, 8, C1)
        for a in range(2):
            found[a, b] = rows[:, a].reshape(16, C1)
    return [found[a, b] for a in range(2) for b in range(2)]


def put_pieces(ref, at, pieces):
    for b in range(2):
        rows = jnp.stack(
            [pieces[b].reshape(2, 8, C1), pieces[2 + b].reshape(2, 8, C1)], axis=1
        ).reshape(32, C1)
        for k in range(4):
            ref[k, pl.ds(at * 64 + b, 32, 2), :] = rows[:, 128 * k : 128 * k + 128]


def joined_rows(ref, at, width):
    return jnp.concatenate([ref[k, block(at, 64)] for k in range(4)], axis=1)


def by_row(x, width):
    x = x.reshape(-1, 2, 8, width)
    return x[:, 0], x[:, 1]


WEIGHTS = dict(
    unmerge=(C2, 4 * C1),
    qkv_one=(C1, 3 * C1),
    proj_one=(C1, C1),
    merge=(4 * C1, C2),
    qkv_two=(C2, 3 * C2),
    proj_two=(C2, C2),
)

BUFFERS = dict(
    window=((TOKENS + 64, C1), BF),
    labels=((8, 128), F32),
    normed_one=((TOKENS, C1), BF),
    packed_one=((TOKENS, 3 * C1), BF),
    expo_one=((32, 256, 128), BF),
    over_one=((32, 128, 128), BF),
    mixed_one=((TOKENS, C1), BF),
    y_shift=((TOKENS, C1), BF),
    outgoing=((TOKENS, C1), BF),
    fine=((COARSE, 4 * C1), BF),
    spare=((4, TOKENS, 128), F32),
    grouped=((COARSE, 4 * C1), BF),
    coarse=((COARSE, C2), BF),
    coarse_rows=((COARSE, C2), BF),
    grad_skip_rows=((COARSE, C2), BF),
    normed_two=((COARSE, C2), BF),
    packed_two=((COARSE, 3 * C2), BF),
    expo_two=((16, 256, 128), BF),
    over_two=((16, 128, 128), BF),
    mixed_two=((COARSE, C2), BF),
    grad_mixed_two=((COARSE, C2), BF),
    wide=((COARSE, C2), F32),
    level_two_rows=((COARSE, C2), BF),
    level_two=((COARSE, C2), BF),
    grad_coarse_rows=((COARSE, C2), BF),
    grad_coarse=((COARSE, C2), BF),
    left_q=((512, 512), BF),
    left_p=((512, 512), BF),
    leave=((2, 512, 256), BF),
    right_q=((2 * COARSE, 3 * C2), BF),
    right_p=((2 * COARSE, C2), BF),
)


def scratch_list():
    shapes = [pltpu.VMEM(shape, BF) for shape in WEIGHTS.values()]
    shapes += [pltpu.VMEM(shape, dtype) for shape, dtype in BUFFERS.values()]
    shapes += [pltpu.SemaphoreType.DMA((len(WEIGHTS),)), pltpu.SemaphoreType.DMA((5,))]
    shapes += [pltpu.SemaphoreType.DMA((4,)), pltpu.SemaphoreType.DMA((4,))]
    shapes += [pltpu.SemaphoreType.DMA((LONS,)) for _ in range(8)]
    for _ in range(4):
        shapes += halo_scratch()
    return shapes + reduce_scratch()


def whole_kernel(*refs):
    region, tokens, cotangent = refs[:3]
    stored = refs[3:9]
    out_ref, grad_ref, qkv_ref, proj_ref = refs[9:13]
    scratch = list(refs[13:])

    def take(count):
        taken = scratch[:count]
        del scratch[:count]
        return taken

    weight = SimpleNamespace(**dict(zip(WEIGHTS, take(len(WEIGHTS)))))
    buf = SimpleNamespace(**dict(zip(BUFFERS, take(len(BUFFERS)))))
    load_sem, field_sem = take(2)
    pair_send, pair_recv = take(2)
    row_sems = [take(2) for _ in range(4)]
    halos = [take(5) for _ in range(4)]
    reducer = Reducer(take(len(reduce_scratch())))
    c = reducer.c
    lat, lon = lax.axis_index("lat"), lax.axis_index("lon")

    partners = [(lat, (lon + by) % LONS) for by in range(1, LONS)]
    for way in (1, -1):
        partners.append(((lat + way) % LATS, lon))
        partners.append(((lat + way) % LATS, (lon + way) % LONS))
    partners += [device_of(moved(c, axis, by)) for axis in ("x", "y", "z") for by in (1, 2, 3)]
    barrier = pltpu.get_barrier_semaphore()
    for partner in partners:
        pl.semaphore_signal(barrier, inc=1, device_id=partner, device_id_type=MESH)

    loads = {
        name: pltpu.make_async_copy(source, getattr(weight, name), load_sem.at[k])
        for k, (name, source) in enumerate(zip(WEIGHTS, stored))
    }
    token_load = pltpu.make_async_copy(tokens, buf.window.at[64:1088], field_sem.at[0])
    cotangent_load = pltpu.make_async_copy(cotangent, buf.mixed_one, field_sem.at[1])
    cotangent_again = pltpu.make_async_copy(cotangent, buf.y_shift, field_sem.at[2])
    output_store = pltpu.make_async_copy(buf.outgoing, out_ref, field_sem.at[3])
    grad_store = pltpu.make_async_copy(buf.outgoing, grad_ref, field_sem.at[4])
    token_load.start()
    cotangent_load.start()
    for copy in loads.values():
        copy.start()
    loads = SimpleNamespace(**loads)

    column = lax.broadcasted_iota(jnp.int32, (16, 128), 0)
    place = lax.broadcasted_iota(jnp.int32, (16, 128), 1) & 15
    chosen = jnp.where(column == ((place + 4) & 15), 1.0, 0.0).astype(BF)
    spread_region = dot_tn(region[...].astype(F32).astype(BF), chosen).reshape(8, 8, 128)
    row = lax.broadcasted_iota(jnp.int32, (8, 8, 128), 1)
    token = lax.broadcasted_iota(jnp.int32, (8, 8, 128), 2)
    own_row = jnp.where(row == (token >> 4), spread_region, 0.0)
    second = jnp.where(((token + 4) & 15) >= 8, 1.0, 0.0)[:, 0]
    buf.labels[...] = jnp.sum(own_row, axis=1) * 2.0 + second

    tokens_in = Halo(buf.window, halos[0], 1, 64)
    fine_back = Halo(buf.y_shift, halos[1], -1)
    grads_in = Halo(buf.normed_one, halos[2], 1)
    grads_back = Halo(buf.y_shift, halos[3], -1)
    skip_to_rows = Rows(buf.grad_mixed_two, buf.grad_skip_rows, row_sems[0])
    coarse_to_rows = Rows(buf.coarse, buf.coarse_rows, row_sems[1])
    level_to_tile = Rows(buf.level_two_rows, buf.level_two, row_sems[2])
    grad_to_tile = Rows(buf.grad_coarse_rows, buf.grad_coarse, row_sems[3])

    with jax.named_scope("tokens_in"):
        token_load.wait()
        tokens_in.pack(0)
        tokens_in.pack(1)
        pl.semaphore_wait(barrier, len(partners))
        tokens_in.start(range(4))

    with jax.named_scope("grad_skip"):
        cotangent_load.wait()

        def spread(at):
            spread_lanes(buf.spare, at, buf.mixed_one[block(at, 64)].astype(F32))

        loop(16, spread)

        def group_cotangent(at):
            buf.grouped[block(at, 16)] = jnp.concatenate(
                fine_pieces(buf.spare, at), axis=1
            ).astype(BF)

        loop(16, group_cotangent)

    def lanes(third, pair):
        return slice(C1 * third + 128 * pair, C1 * third + 128 * pair + 128)

    def windows_allowed(group):
        row = jnp.broadcast_to(buf.labels[pl.ds(group, 1), :], (128, 128))
        return row == row.T

    with jax.named_scope("level_one"):
        def write_window(at, rows):
            buf.window[block(at, 64)] = rows.astype(BF)
            buf.normed_one[block(at, 64)] = normalised(rows)[0].astype(BF)

        loads.qkv_one.wait()
        loads.proj_one.wait()
        for half in range(2):
            tokens_in.wait((3,) if half else (0, 1, 2))
            tokens_in.assemble(half, write_window)
            rows = slice(512 * half, 512 * half + 512)

            def project(at):
                buf.packed_one[rows, block(at, 256)] = dot(
                    buf.normed_one[rows], weight.qkv_one[:, block(at, 256)]
                ).astype(BF)

            loop(6, project, DENSE)

            def attend_group(at):
                group = at + 4 * half
                where = block(group, 128)
                units = [
                    [buf.packed_one[where, lanes(third, pair)] for third in range(3)]
                    for pair in range(4)
                ]
                for pair, found in enumerate(attend(units, windows_allowed(group))):
                    at_unit = group * 4 + pair
                    buf.expo_one[at_unit], buf.over_one[at_unit], mixed = found
                    buf.mixed_one[where, lanes(0, pair)] = mixed

            loop(4, attend_group, HEADS)

            def add_tokens(at):
                columns = block(at, 256)
                buf.y_shift[rows, columns] = (
                    buf.window[rows, columns].astype(F32)
                    + dot(buf.mixed_one[rows], weight.proj_one[:, columns])
                ).astype(BF)

            loop(2, add_tokens, DENSE)
            fine_back.pack(half)
            fine_back.start((0, 1, 2) if half == 0 else (3,))

    with jax.named_scope("merge"):
        loads.unmerge.wait()

        def grad_skip(at):
            buf.grad_mixed_two[:, block(at, 256)] = dot_nt(
                buf.grouped[...], weight.unmerge[block(at, 256)]
            ).astype(BF)

        loop(4, grad_skip, DENSE)
        skip_to_rows.start(0)
        skip_to_rows.start(1)

        def write_fine(at, rows):
            spread_lanes(buf.spare, at, rows.astype(BF).astype(F32))

        def group_fine(at):
            whole = jnp.concatenate(fine_pieces(buf.spare, at), axis=1)
            buf.fine[block(at, 16)] = whole.astype(BF)
            buf.grouped[block(at, 16)] = normalised(whole)[0].astype(BF)

        fine_back.wait((0, 1, 2))
        fine_back.assemble(0, write_fine)
        loop(8, lambda at: group_fine((at + 15) % 16))
        fine_back.wait((3,))
        fine_back.assemble(1, write_fine)
        loop(8, lambda at: group_fine(at + 7))
        loads.merge.wait()

        for half in range(2):
            rows = slice(128 * half, 128 * half + 128)

            def merge(at):
                columns = block(at, 256)
                buf.coarse[rows, columns] = dot(
                    buf.grouped[rows], weight.merge[:, columns]
                ).astype(BF)

            loop(4, merge, DENSE)
            coarse_to_rows.start(half)
        fine_back.drain()
        cotangent_again.start()

    with jax.named_scope("level_two"):
        loads.qkv_two.wait()
        loads.proj_two.wait()
        coarse_to_rows.wait()

        def norm_two(at):
            both = by_row(buf.coarse_rows[block(at, 64)].astype(F32), C2)
            for row in range(2):
                x = both[row].reshape(32, C2)
                where = pl.ds(pl.multiple_of(at * 32 + 128 * row, 32), 32)
                buf.wide[where] = x
                buf.normed_two[where] = normalised(x)[0].astype(BF)

        loop(4, norm_two)

        def project_two(at):
            columns = block(at, 256)
            buf.packed_two[:, columns] = dot(
                buf.normed_two[...], weight.qkv_two[:, columns]
            ).astype(BF)

        loop(12, project_two, DENSE)

        def operands_two(row, pair):
            rows = slice(128 * row, 128 * row + 128)
            return [
                buf.packed_two[rows, pl.ds(pl.multiple_of(C2 * third + pair * 128, 128), 128)]
                for third in range(3)
            ]

        def attend_two(at):
            places = [(2 * at + k, row) for k in range(2) for row in range(2)]
            units = [operands_two(row, pair) for pair, row in places]
            for (pair, row), found in zip(places, attend(units, None)):
                at_unit = pair * 2 + row
                buf.expo_two[at_unit], buf.over_two[at_unit], mixed = found
                buf.mixed_two[128 * row : 128 * row + 128, block(pair, 128)] = mixed

        loop(4, attend_two, HEADS)

        def add_coarse(at):
            columns = block(at, 256)
            total = buf.wide[:, columns] + dot(buf.mixed_two[...], weight.proj_two[:, columns])
            buf.level_two_rows[:, columns] = (
                jnp.stack([total[:128].reshape(16, 8, 256), total[128:].reshape(16, 8, 256)], axis=1)
                .reshape(256, 256)
                .astype(BF)
            )

        loop(4, add_coarse, DENSE)
        level_to_tile.start(0)
        level_to_tile.start(1)

    pair_copies = [
        remote(source, target, pair_send.at[k], pair_recv.at[k], device_of(moved(c, "core", 1)))
        for k, (source, target) in enumerate(
            (
                (buf.right_q.at[0:256], buf.right_q.at[256:512]),
                (buf.right_p.at[0:256], buf.right_p.at[256:512]),
                (buf.leave.at[0], buf.left_q.at[:, 256:512]),
                (buf.leave.at[1], buf.left_p.at[:, 256:512]),
            )
        )
    ]

    with jax.named_scope("grad_level_two"):
        skip_to_rows.wait()

        def grad_level(at):
            x = buf.level_two_rows[block(at, 64)].astype(F32)
            g = buf.grad_skip_rows[block(at, 64)].astype(F32)
            both = by_row(norm_back(x, g), C2)
            for row in range(2):
                where = pl.ds(pl.multiple_of(at * 32 + 128 * row, 32), 32)
                buf.right_p[where] = both[row].reshape(32, C2).astype(BF)

        loop(4, grad_level)
        pair_copies[1].start()
        skip_to_rows.drain()

        def grad_mixed(at):
            buf.grad_mixed_two[:, block(at, 256)] = dot_nt(
                buf.right_p[0:256], weight.proj_two[block(at, 256)]
            ).astype(BF)

        loop(4, grad_mixed, DENSE)

        def attend_two_back(at):
            places = [(2 * at + k, row) for k in range(2) for row in range(2)]
            units = []
            for pair, row in places:
                rows = slice(128 * row, 128 * row + 128)
                units.append(
                    operands_two(row, pair)
                    + [
                        buf.expo_two[pair * 2 + row],
                        buf.over_two[pair * 2 + row],
                        buf.mixed_two[rows, block(pair, 128)],
                        buf.grad_mixed_two[rows, block(pair, 128)],
                    ]
                )
            for (pair, row), found in zip(places, attend_back(units)):
                for third in range(3):
                    where = pl.ds(pl.multiple_of(C2 * third + pair * 128, 128), 128)
                    buf.right_q[128 * row : 128 * row + 128, where] = found[third]

        loop(4, attend_two_back, HEADS)

    def turn(source, left, slot):
        first = c["core"] == 0
        for half in range(2):
            tokens_at = slice(128 * half, 128 * half + 128)
            groups = source[tokens_at].astype(F32).T.reshape(64, 2, 8, 128)
            mine = jnp.where(first, groups[:, 0], groups[:, 1])
            theirs = jnp.where(first, groups[:, 1], groups[:, 0])
            left[:, tokens_at] = mine.reshape(512, 128).astype(BF)
            buf.leave[slot, :, tokens_at] = theirs.reshape(512, 128).astype(BF)

    with jax.named_scope("grad_coarse"):
        pair_copies[0].start()

        def grad_normed_two(at):
            buf.grad_mixed_two[:, block(at, 256)] = dot_nt(
                buf.right_q[0:256], weight.qkv_two[block(at, 256)]
            ).astype(BF)

        loop(4, grad_normed_two, DENSE)

        def grad_coarse(at):
            both = []
            for row in range(2):
                where = pl.ds(pl.multiple_of(at * 32 + 128 * row, 32), 32)
                g = norm_back(buf.wide[where], buf.grad_mixed_two[where].astype(F32))
                g = g.astype(BF).astype(F32) + buf.right_p[where].astype(F32)
                both.append(g.reshape(4, 8, C2))
            buf.grad_coarse_rows[block(at, 64)] = (
                jnp.stack(both, axis=1).reshape(64, C2).astype(BF)
            )

        for half in range(2):
            loop(2, lambda at: grad_coarse(at + 2 * half))
            grad_to_tile.start(half)

    with jax.named_scope("weight_gradients"):
        turn(buf.normed_two, buf.left_q, 0)
        pair_copies[2].start()
        turn(buf.mixed_two, buf.left_p, 1)
        pair_copies[3].start()
        for copy in pair_copies:
            copy.wait_recv()

        def put_total(zh, columns, top, low):
            width = top.shape[1]
            both = jnp.concatenate([top.reshape(32, 8, width), low.reshape(32, 8, width)], axis=1)
            reducer.total[zh, :, :, :, :, columns] = both.astype(BF).reshape(4, 2, 4, 16, width)

        def narrow_tile(at):
            right = jnp.concatenate(
                [buf.right_q[:, block(at, 128)], buf.right_q[:, block(at + 16, 128)]], axis=1
            )
            for zh in range(2):
                both = dot(buf.left_q[256 * zh : 256 * zh + 256], right)
                put_total(zh, block(at, 128), both[:, :128], both[:, 128:])

        def wide_tile(at):
            for zh in range(2):
                rows = slice(256 * zh, 256 * zh + 256)
                top = dot(buf.left_q[rows], buf.right_q[:, block(at, 256)])
                low = dot(buf.left_p[rows], buf.right_p[:, block(at - 4, 256)])
                put_total(zh, block(at, 256), top, low)

        for part, (start, stop, _) in enumerate(PARTS):
            middle = max(start, min(stop, 1024))
            if middle > start:
                loop((middle - start) // 128, lambda at: narrow_tile(at + start // 128), TILES)
            if stop > middle:
                loop((stop - middle) // 256, lambda at: wide_tile(at + middle // 256), TILES)
            reducer.start(part, 0)

    with jax.named_scope("grad_fine"):
        grad_to_tile.wait()

        def grad_grouped(at):
            buf.grouped[:, block(at, 256)] = dot_nt(
                buf.grad_coarse[...], weight.merge[block(at, 256)]
            ).astype(BF)

        loop(8, grad_grouped, DENSE)
        for part in range(3):
            reducer.pass_on(part)

        def grad_pieces(at):
            g = norm_back(
                buf.fine[block(at, 16)].astype(F32), buf.grouped[block(at, 16)].astype(F32)
            )
            put_pieces(buf.spare, at, [g[:, C1 * k : C1 * k + C1] for k in range(4)])

        loop(16, grad_pieces)

        cotangent_again.wait()

        def grad_fine(at):
            buf.normed_one[block(at, 64)] = (
                joined_rows(buf.spare, at, C1) + buf.y_shift[block(at, 64)].astype(F32)
            ).astype(BF)

        loop(16, grad_fine)
        grads_in.pack(0)
        grads_in.pack(1)
        grads_in.start(range(4))

    with jax.named_scope("output"):
        level_to_tile.wait()

        def norm_level(at):
            x = buf.level_two[block(at, 64)].astype(F32)
            buf.coarse[block(at, 64)] = normalised(x)[0].astype(BF)

        coarse_to_rows.drain()
        loop(4, norm_level)

        for half in range(2):
            rows = slice(128 * half, 128 * half + 128)

            def unmerge(at):
                for low in range(2):
                    buf.wide[128 * low : 128 * low + 128, block(at, 256)] = dot(
                        buf.coarse[rows], weight.unmerge[:, block(at + 4 * low, 256)]
                    )

            loop(4, unmerge, DENSE)

            def add_fine(at):
                fine = buf.fine[block(at + 8 * half, 16)].astype(F32)
                upper = jnp.concatenate(
                    [buf.wide[block(at, 16)], buf.wide[block(at + 8, 16)]], axis=1
                )
                total = fine + upper
                put_pieces(
                    buf.spare,
                    at + 8 * half,
                    [total[:, C1 * k : C1 * k + C1] for k in range(4)],
                )

            loop(8, add_fine)

        def write_output(at):
            buf.outgoing[block(at, 64)] = joined_rows(buf.spare, at, C1).astype(BF)

        loop(16, write_output)
        output_store.start()

    with jax.named_scope("grad_level_one"):

        def write_grads(at, rows):
            buf.y_shift[block(at, 64)] = rows.astype(BF)

        for half in range(2):
            grads_in.wait((3,) if half else (0, 1, 2))
            grads_in.assemble(half, write_grads)
            if half:
                grads_in.drain()
            rows = slice(512 * half, 512 * half + 512)

            def grad_mixed_one(at):
                buf.normed_one[rows, block(at, 256)] = dot_nt(
                    buf.y_shift[rows], weight.proj_one[block(at, 256)]
                ).astype(BF)

            loop(2, grad_mixed_one, DENSE)

            def attend_group_back(at):
                group = at + 4 * half
                where = block(group, 128)
                units = []
                for pair in range(4):
                    at_unit = group * 4 + pair
                    units.append(
                        [buf.packed_one[where, lanes(third, pair)] for third in range(3)]
                        + [
                            buf.expo_one[at_unit],
                            buf.over_one[at_unit],
                            buf.mixed_one[where, lanes(0, pair)],
                            buf.normed_one[where, lanes(0, pair)],
                        ]
                    )
                for pair, found in enumerate(attend_back(units)):
                    for third in range(3):
                        buf.packed_one[where, lanes(third, pair)] = found[third]

            loop(4, attend_group_back, HEADS)
            for part in range(3):
                reducer.finish(part, half)
                reducer.start(part, half + 1)

            def grad_normed_one(at):
                buf.normed_one[rows, block(at, 256)] = dot_nt(
                    buf.packed_one[rows], weight.qkv_one[block(at, 256)]
                ).astype(BF)

            loop(2, grad_normed_one, DENSE)

            def grad_window(at):
                where = block(at + 8 * half, 64)
                g = norm_back(
                    buf.window[where].astype(F32), buf.normed_one[where].astype(F32)
                )
                buf.y_shift[where] = (g + buf.y_shift[where].astype(F32)).astype(BF)

            loop(8, grad_window)
            grads_back.pack(half)
            grads_back.start((0, 1, 2) if half == 0 else (3,))

    with jax.named_scope("grad_tokens"):
        output_store.wait()

        def write_tokens(at, rows):
            buf.outgoing[block(at, 64)] = rows.astype(BF)

        grads_back.wait((0, 1, 2))
        grads_back.assemble(0, write_tokens)
        grads_back.wait((3,))
        grads_back.assemble(1, write_tokens)
        grad_store.start()
        for part in range(3):
            store_folded(part, reducer.finish(part, 2), qkv_ref, proj_ref)

    tokens_in.drain()
    grads_back.drain()
    level_to_tile.drain()
    grad_to_tile.drain()
    for copy in pair_copies:
        copy.wait_send()
    reducer.drain()
    grad_store.wait()


def hand_over(*refs):
    for source, target in zip(refs[:4], refs[4:]):
        target[...] = source[...]


def body(
    tokens, region, qkv_one, proj_one, merge_weight, qkv_two, proj_two, unmerge_weight, cotangent
):
    vmem = pl.BlockSpec(memory_space=pltpu.VMEM)
    anywhere = pl.BlockSpec(memory_space=pl.ANY)
    shapes = (
            jax.ShapeDtypeStruct((TOKENS, C1), BF),
            jax.ShapeDtypeStruct((TOKENS, C1), BF),
            jax.ShapeDtypeStruct((8, 3 * C2), F32),
            jax.ShapeDtypeStruct((8, C2), F32),
    )
    found = pl.pallas_call(
        whole_kernel,
        out_shape=shapes,
        in_specs=[vmem] + [anywhere] * 8,
        out_specs=(anywhere, anywhere, vmem, vmem),
        scratch_shapes=scratch_list(),
        compiler_params=pltpu.CompilerParams(
            collective_id=0, has_side_effects=True, vmem_limit_bytes=VMEM_LIMIT
        ),
    )(
        region.T,
        tokens.reshape(TOKENS, C1),
        cotangent.reshape(TOKENS, C1),
        unmerge_weight,
        qkv_one,
        proj_one,
        merge_weight,
        qkv_two,
        proj_two,
    )
    pieces = [
        pl.BlockSpec((TOKENS // 2, C1), lambda at: (at, 0)),
        pl.BlockSpec((TOKENS // 2, C1), lambda at: (at, 0)),
        pl.BlockSpec((8, 3 * C2 // 2), lambda at: (0, at)),
        pl.BlockSpec((8, C2 // 2), lambda at: (0, at)),
    ]
    output, grad_tokens, grad_qkv_two, grad_proj_two = pl.pallas_call(
        hand_over, grid=(2,), out_shape=shapes, in_specs=pieces, out_specs=pieces
    )(*found)
    shape = tokens.shape
    return output.reshape(shape), grad_tokens.reshape(shape), grad_qkv_two, grad_proj_two


def solution(mesh):
    return jax.shard_map(
        body,
        mesh=mesh,
        in_specs=(
            P("lat", "lon", None),
            P("lat", "lon"),
            P(),
            P(),
            P(),
            P(),
            P(),
            P(),
            P("lat", "lon", None),
        ),
        out_specs=(
            P("lat", "lon", None),
            P("lat", "lon", None),
            P(("lat", "lon"), None),
            P(("lat", "lon"), None),
        ),
        check_vma=False,
    )
```

```python
import itertools
from types import SimpleNamespace

import jax
import jax.numpy as jnp
from jax import lax
from jax.experimental import pallas as pl
from jax.experimental.pallas import tpu as pltpu
from jax.sharding import PartitionSpec as P

MESH = pl.DeviceIdType.MESH
BF = jnp.bfloat16
F32 = jnp.float32
VMEM_LIMIT = 63 * 1024 * 1024

TOKENS, C1, C2 = 1024, 512, 1024
COARSE = 256
LONS, LATS = 16, 8
DENSE, HEADS, TILES = 4, 1, 5

FOLD = 2048
PARTS = ((0, 640, ("x", "y", "z")), (640, 1280, ("y", "z", "x")), (1280, 2048, ("z", "x", "y")))
LABELS = ("zh", "x", "zl", "y")


def coordinates():
    lat, lon = lax.axis_index("lat"), lax.axis_index("lon")
    return {
        "zh": lat // 4,
        "x": lat % 4,
        "zl": lon // 8,
        "y": (lon // 2) % 4,
        "core": lon % 2,
    }


def device_of(c):
    return (c["zh"] * 4 + c["x"], (c["zl"] * 4 + c["y"]) * 2 + c["core"])


def moved(c, axis, by):
    c = dict(c)
    if axis == "z":
        z = (c["zh"] * 2 + c["zl"] + by) % 4
        c["zh"], c["zl"] = z // 2, z % 2
    elif axis == "core":
        c["core"] = 1 - c["core"]
    else:
        c[axis] = (c[axis] + by) % 4
    return c


def pick(labels, axis, c):
    names = ("zh", "zl") if axis == "z" else (axis,)
    return tuple(c[label] if label in names else slice(None) for label in labels)


def drop(labels, axis):
    names = ("zh", "zl") if axis == "z" else (axis,)
    return tuple(label for label in labels if label not in names)


def sizes(labels):
    return tuple(4 if label in ("x", "y") else 2 for label in labels)


def remote(source, target, send_sem, recv_sem, device):
    return pltpu.make_async_remote_copy(
        src_ref=source,
        dst_ref=target,
        send_sem=send_sem,
        recv_sem=recv_sem,
        device_id=device,
        device_id_type=MESH,
    )


def reduce_scratch():
    shapes = [pltpu.VMEM((2, 4, 2, 4, 16, FOLD), BF)]
    for start, stop, order in PARTS:
        labels = LABELS
        for step, axis in enumerate(order):
            labels = drop(labels, axis)
            shapes.append(pltpu.VMEM((3,) + sizes(labels) + (16, stop - start), BF))
            if step < 2:
                shapes.append(pltpu.VMEM(sizes(labels) + (16, stop - start), BF))
    shapes += [pltpu.SemaphoreType.DMA((3, 3, 3)), pltpu.SemaphoreType.DMA((3, 3, 3))]
    return shapes + [pltpu.SemaphoreType.DMA((3, 6)), pltpu.SemaphoreType.DMA((3, 6))]


class Reducer:
    def __init__(self, scratch):
        self.total = scratch[0]
        self.slots = [scratch[1 + 5 * p : 6 + 5 * p] for p in range(3)]
        self.send_sem, self.recv_sem, self.ring_send, self.ring_recv = scratch[16:]
        self.c = coordinates()

    def source(self, part, step):
        start, stop, order = PARTS[part]
        labels = LABELS
        for axis in order[:step]:
            labels = drop(labels, axis)
        if step == 0:
            return labels, self.total, (slice(None), pl.ds(start, stop - start))
        return labels, self.slots[part][2 * step - 1], (slice(None), slice(None))

    def copies(self, part, step):
        axis = PARTS[part][2][step]
        labels, source, rest = self.source(part, step)
        found = []
        for by in (2, 1, 3):
            target = moved(self.c, axis, by)
            found.append(
                remote(
                    source.at[pick(labels, axis, target) + rest],
                    self.slots[part][2 * step].at[by - 1],
                    self.send_sem.at[part, step, by - 1],
                    self.recv_sem.at[part, step, by - 1],
                    device_of(target),
                )
            )
        return found

    def ring(self, part):
        start, stop, order = PARTS[part]
        axis, width = order[0], stop - start
        cut = width // 256 * 128
        halves = ((0, cut), (cut, width - cut))
        after, before, opposite = (moved(self.c, axis, by) for by in (1, 3, 2))
        every = (slice(None),) * len(drop(LABELS, axis))

        def mine(owner, half):
            at, size = halves[half]
            return self.total.at[pick(LABELS, axis, owner) + (slice(None), pl.ds(start + at, size))]

        def slot(which, half):
            at, size = halves[half]
            return self.slots[part][0].at[(which,) + every + (slice(None), pl.ds(at, size))]

        plan = (
            (mine(opposite, 0), slot(2, 0), after),
            (mine(opposite, 1), slot(2, 1), before),
            (mine(after, 1), slot(0, 1), after),
            (mine(before, 0), slot(1, 0), before),
            (slot(2, 0), slot(0, 0), after),
            (slot(2, 1), slot(1, 1), before),
        )
        copies = [
            remote(source, target, self.ring_send.at[part, k], self.ring_recv.at[part, k], device_of(device))
            for k, (source, target, device) in enumerate(plan)
        ]
        return copies, halves, (after, before)

    def start(self, part, step):
        copies = self.copies(part, step) if step else self.ring(part)[0][:4]
        for copy in copies:
            copy.start()

    def pass_on(self, part):
        copies, halves, owners = self.ring(part)
        start, _, order = PARTS[part]
        left = drop(LABELS, order[0])
        passed = self.slots[part][0]
        for half, (at, size) in enumerate(halves):
            copies[half].wait_recv()
            for place in itertools.product(*[range(count) for count in sizes(left)]):
                where = {**owners[half], **dict(zip(left, place))}
                own = self.total[
                    tuple(where[label] for label in LABELS) + (slice(None), slice(start + at, start + at + size))
                ]
                here = (2,) + place + (slice(None), slice(at, at + size))
                passed[here] = (passed[here].astype(F32) + own.astype(F32)).astype(BF)
            copies[4 + half].start()

    def finish(self, part, step):
        copies = self.copies(part, step) if step else self.ring(part)[0][2:]
        for copy in copies:
            copy.wait_recv()
        axis = PARTS[part][2][step]
        labels, source, rest = self.source(part, step)
        arrived = self.slots[part][2 * step]
        left = drop(labels, axis)
        for place in itertools.product(*[range(size) for size in sizes(left)]):
            where = dict(zip(left, place))
            where.update({k: self.c[k] for k in labels if k not in where})
            own = source[tuple(where[label] for label in labels) + rest].astype(F32)
            summed = own
            for slot in range(3 if step else 2):
                summed = summed + arrived[(slot,) + place].astype(F32)
            if step == 2:
                return summed
            self.slots[part][2 * step + 1][place] = summed.astype(BF)

    def drain(self):
        for part in range(3):
            for copy in self.ring(part)[0]:
                copy.wait_send()
            for step in range(1, 3):
                for copy in self.copies(part, step):
                    copy.wait_send()


def store_folded(part, summed, qkv_ref, proj_ref):
    start, stop, _ = PARTS[part]
    top, low = summed[:8], summed[8:]
    qkv_ref[:, start:stop] = top
    cut = min(max(1024 - start, 0), stop - start)
    if cut:
        qkv_ref[:, FOLD + start : FOLD + start + cut] = low[:, :cut]
    if cut < stop - start:
        proj_ref[:, start + cut - 1024 : stop - 1024] = low[:, cut:]


def block(at, size):
    return pl.ds(pl.multiple_of(at * size, size), size)


def loop(count, body, most=4):
    size = max(k for k in range(1, most + 1) if count % k == 0)

    def turn(at, carry):
        for k in range(size):
            body(at * size + k)
        return carry

    lax.fori_loop(0, count // size, turn, 0)


def dot(a, b):
    return jnp.dot(a, b, preferred_element_type=F32)


def dot_nt(a, b):
    return lax.dot_general(a, b, (((1,), (1,)), ((), ())), preferred_element_type=F32)


def dot_tn(a, b):
    return lax.dot_general(a, b, (((0,), (0,)), ((), ())), preferred_element_type=F32)


def normalised(x):
    centered = x - jnp.mean(x, axis=-1, keepdims=True)
    spread = jnp.mean(centered * centered, axis=-1, keepdims=True)
    scale = lax.rsqrt(spread + 1e-05)
    return centered * scale, scale


def norm_back(x, g):
    hat, scale = normalised(x)
    return scale * (
        g - jnp.mean(g, axis=-1, keepdims=True) - hat * jnp.mean(g * hat, axis=-1, keepdims=True)
    )


def by_head(pair, scale=1.0):
    lane = lax.broadcasted_iota(jnp.int32, (1, 128), 1)
    first = jnp.where(lane < 64, scale, 0.0).astype(BF)
    second = jnp.where(lane < 64, 0.0, scale).astype(BF)
    return jnp.concatenate([pair * first, pair * second], axis=0)


def side_by_side(stacked):
    return jnp.concatenate([stacked[:128], stacked[128:]], axis=1)


def attend(units, allowed):
    ones = by_head(jnp.ones((128, 128), BF))
    scores = [dot_nt(by_head(q, 0.125), k) for q, k, _ in units]
    if allowed is not None:
        scores = [
            jnp.where(allowed[None], one.reshape(2, 128, 128), -1e30).reshape(256, 128)
            for one in scores
        ]
    expo = [jnp.exp(one - jnp.max(one, axis=-1, keepdims=True)).astype(BF) for one in scores]
    found = []
    for one, (_, _, v) in zip(expo, units):
        both = dot(side_by_side(one), jnp.concatenate([by_head(v), ones], axis=1))
        over = 1.0 / both[:, 128:]
        found.append((one, over.astype(BF), (both[:, :128] * over).astype(BF)))
    return found


def attend_back(units):
    minus = jnp.full((128, 128), -1.0, BF)
    found = []
    for q, k, v, expo, over, mixed, g in units:
        g = g * over
        both = by_head(g)
        change = dot_nt(
            jnp.concatenate([both, by_head(g * mixed)], axis=1),
            jnp.concatenate([v, minus], axis=1),
        )
        grad_scores = (expo.astype(F32) * change).astype(BF)
        grad_q = dot(side_by_side(grad_scores), by_head(k, 0.125))
        grad_k = dot_tn(grad_scores, by_head(q, 0.125))
        grad_v = dot_tn(expo, both)
        found.append((grad_q.astype(BF), grad_k.astype(BF), grad_v.astype(BF)))
    return found


def pack_columns(rows):
    n = rows.shape[0] // 32
    width = rows.shape[1]
    late = rows.reshape(n, 2, 16, width)[:, :, 8:, :]
    place = lax.broadcasted_iota(jnp.int32, (n, 8, width), 1)
    both = jnp.where(place < 4, pltpu.roll(late[:, 0], 4, 1), late[:, 1])
    return both.reshape(n * 8, width).astype(BF)


def put_columns(rows, packed):
    n = rows.shape[0] // 32
    width = rows.shape[1]
    pairs = rows.reshape(n, 2, 16, width)
    arrived = packed.astype(F32).reshape(n, 8, width)
    place = lax.broadcasted_iota(jnp.int32, (n, 8, width), 1)
    even = jnp.where(place >= 4, pltpu.roll(arrived, 4, 1), pairs[:, 0, 8:])
    odd = jnp.where(place >= 4, arrived, pairs[:, 1, 8:])
    whole = jnp.concatenate([pairs[:, 0, :8], even, pairs[:, 1, :8], odd], axis=1)
    return whole.reshape(n * 32, width)


class Halo:

    def __init__(self, field, scratch, way, start=0):
        self.field, self.first = field, start
        self.packed, self.columns, self.rows, self.send_sem, self.recv_sem = scratch
        self.way = way

    def pack(self, half):
        def body(at):
            at = at + 4 * half
            rows = self.field[pl.ds(pl.multiple_of(at * 128 + self.first, 64), 128)]
            self.packed[block(at, 32)] = pack_columns(rows.astype(F32))

        loop(4, body)

    def copies(self):
        lat, lon = lax.axis_index("lat"), lax.axis_index("lon")
        way = self.way
        lat_to, lon_to = (lat + way) % LATS, (lon + way) % LONS
        if way == 1:
            plan = (
                (self.field.at[self.first + 960 : self.first + 1024], self.rows.at[:], (lat_to, lon)),
                (self.packed.at[240:256], self.columns.at[0:16], (lat_to, lon_to)),
                (self.packed.at[0:128], self.columns.at[16:144], (lat, lon_to)),
                (self.packed.at[128:240], self.columns.at[144:256], (lat, lon_to)),
            )
        else:
            plan = (
                (self.field.at[0:64], self.rows.at[:], (lat_to, lon)),
                (self.packed.at[0:16], self.columns.at[240:256], (lat_to, lon_to)),
                (self.packed.at[16:128], self.columns.at[0:112], (lat, lon_to)),
                (self.packed.at[128:256], self.columns.at[112:240], (lat, lon_to)),
            )
        return [
            remote(source, target, self.send_sem.at[k], self.recv_sem.at[k], device)
            for k, (source, target, device) in enumerate(plan)
        ]

    def start(self, which):
        copies = self.copies()
        for k in which:
            copies[k].start()

    def wait(self, which):
        copies = self.copies()
        for k in which:
            copies[k].wait_recv()

    def drain(self):
        for copy in self.copies():
            copy.wait_send()

    def assemble(self, part, write):
        if self.way == 1:
            if part == 0:
                write(0, put_columns(self.rows[...].astype(F32), self.columns[0:16]))

            def patch(at):
                at = at + 8 * part
                rows = self.field[pl.ds(pl.multiple_of(at * 64 + self.first, 64), 64)]
                write(at + 1, put_columns(rows.astype(F32), self.columns[block(at + 1, 16)]))

            loop(7 if part else 8, patch, 8)
        else:
            if part == 0:
                write(15, put_columns(self.rows[...].astype(F32), self.columns[240:256]))

            def patch(at):
                at = at + 7 * part
                rows = self.field[block(at + 1, 64)]
                write(at, put_columns(rows.astype(F32), self.columns[block(at, 16)]))

            loop(8 if part else 7, patch, 8)


def halo_scratch():
    return [
        pltpu.VMEM((256, C1), BF),
        pltpu.VMEM((256, C1), BF),
        pltpu.VMEM((64, C1), BF),
        pltpu.SemaphoreType.DMA((4,)),
        pltpu.SemaphoreType.DMA((4,)),
    ]


class Rows:

    def __init__(self, source, target, sems):
        self.source, self.target = source, target
        self.send_sem, self.recv_sem = sems

    def copy(self, by):
        lat, lon = lax.axis_index("lat"), lax.axis_index("lon")
        to = (lon + by) % LONS
        return remote(
            self.source.at[block(to, 16)],
            self.target.at[block(lon, 16)],
            self.send_sem.at[by],
            self.recv_sem.at[by],
            (lat, to),
        )

    def start_to(self, to):
        lon = lax.axis_index("lon")
        by = (to - lon + LONS) % LONS

        @pl.when(by != 0)
        def _():
            self.copy(by).start()

        @pl.when(by == 0)
        def _():
            self.target[block(lon, 16)] = self.source[block(lon, 16)]

    def start(self, half):
        loop(8, lambda at: self.start_to(at + 8 * half), 1)

    def wait(self):
        loop(15, lambda at: self.copy(at + 1).wait_recv(), 1)

    def drain(self):
        loop(15, lambda at: self.copy(at + 1).wait_send(), 1)


def spread_lanes(ref, at, rows):
    for k in range(4):
        ref[k, block(at, 64)] = rows[:, 128 * k : 128 * k + 128]


def fine_pieces(ref, at):
    found = {}
    for b in range(2):
        lanes = [ref[k, pl.ds(at * 64 + b, 32, 2), :] for k in range(4)]
        rows = jnp.concatenate(lanes, axis=1).reshape(2, 2, 8, C1)
        for a in range(2):
            found[a, b] = rows[:, a].reshape(16, C1)
    return [found[a, b] for a in range(2) for b in range(2)]


def put_pieces(ref, at, pieces):
    for b in range(2):
        rows = jnp.stack(
            [pieces[b].reshape(2, 8, C1), pieces[2 + b].reshape(2, 8, C1)], axis=1
        ).reshape(32, C1)
        for k in range(4):
            ref[k, pl.ds(at * 64 + b, 32, 2), :] = rows[:, 128 * k : 128 * k + 128]


def joined_rows(ref, at, width):
    return jnp.concatenate([ref[k, block(at, 64)] for k in range(4)], axis=1)


def by_row(x, width):
    x = x.reshape(-1, 2, 8, width)
    return x[:, 0], x[:, 1]


WEIGHTS = dict(
    unmerge=(C2, 4 * C1),
    qkv_one=(C1, 3 * C1),
    proj_one=(C1, C1),
    merge=(4 * C1, C2),
    qkv_two=(C2, 3 * C2),
    proj_two=(C2, C2),
)

BUFFERS = dict(
    window=((TOKENS + 64, C1), BF),
    labels=((8, 128), F32),
    normed_one=((TOKENS, C1), BF),
    packed_one=((TOKENS, 3 * C1), BF),
    expo_one=((32, 256, 128), BF),
    over_one=((32, 128, 128), BF),
    mixed_one=((TOKENS, C1), BF),
    y_shift=((TOKENS, C1), BF),
    outgoing=((TOKENS, C1), BF),
    fine=((COARSE, 4 * C1), BF),
    spare=((4, TOKENS, 128), F32),
    grouped=((COARSE, 4 * C1), BF),
    coarse=((COARSE, C2), BF),
    coarse_rows=((COARSE, C2), BF),
    grad_skip_rows=((COARSE, C2), BF),
    normed_two=((COARSE, C2), BF),
    packed_two=((COARSE, 3 * C2), BF),
    expo_two=((16, 256, 128), BF),
    over_two=((16, 128, 128), BF),
    mixed_two=((COARSE, C2), BF),
    grad_mixed_two=((COARSE, C2), BF),
    wide=((COARSE, C2), F32),
    level_two_rows=((COARSE, C2), BF),
    level_two=((COARSE, C2), BF),
    grad_coarse_rows=((COARSE, C2), BF),
    grad_coarse=((COARSE, C2), BF),
    left_q=((512, 512), BF),
    left_p=((512, 512), BF),
    leave=((2, 512, 256), BF),
    right_q=((2 * COARSE, 3 * C2), BF),
    right_p=((2 * COARSE, C2), BF),
)


def scratch_list():
    shapes = [pltpu.VMEM(shape, BF) for shape in WEIGHTS.values()]
    shapes += [pltpu.VMEM(shape, dtype) for shape, dtype in BUFFERS.values()]
    shapes += [pltpu.SemaphoreType.DMA((len(WEIGHTS),)), pltpu.SemaphoreType.DMA((5,))]
    shapes += [pltpu.SemaphoreType.DMA((4,)), pltpu.SemaphoreType.DMA((4,))]
    shapes += [pltpu.SemaphoreType.DMA((LONS,)) for _ in range(8)]
    for _ in range(4):
        shapes += halo_scratch()
    return shapes + reduce_scratch()


def whole_kernel(*refs):
    region, tokens, cotangent = refs[:3]
    stored = refs[3:9]
    out_ref, grad_ref, qkv_ref, proj_ref = refs[9:13]
    scratch = list(refs[13:])

    def take(count):
        taken = scratch[:count]
        del scratch[:count]
        return taken

    weight = SimpleNamespace(**dict(zip(WEIGHTS, take(len(WEIGHTS)))))
    buf = SimpleNamespace(**dict(zip(BUFFERS, take(len(BUFFERS)))))
    load_sem, field_sem = take(2)
    pair_send, pair_recv = take(2)
    row_sems = [take(2) for _ in range(4)]
    halos = [take(5) for _ in range(4)]
    reducer = Reducer(take(len(reduce_scratch())))
    c = reducer.c
    lat, lon = lax.axis_index("lat"), lax.axis_index("lon")

    partners = [(lat, (lon + by) % LONS) for by in range(1, LONS)]
    for way in (1, -1):
        partners.append(((lat + way) % LATS, lon))
        partners.append(((lat + way) % LATS, (lon + way) % LONS))
    partners += [device_of(moved(c, axis, by)) for axis in ("x", "y", "z") for by in (1, 2, 3)]
    barrier = pltpu.get_barrier_semaphore()
    for partner in partners:
        pl.semaphore_signal(barrier, inc=1, device_id=partner, device_id_type=MESH)

    loads = {
        name: pltpu.make_async_copy(source, getattr(weight, name), load_sem.at[k])
        for k, (name, source) in enumerate(zip(WEIGHTS, stored))
    }
    token_load = pltpu.make_async_copy(tokens, buf.window.at[64:1088], field_sem.at[0])
    cotangent_load = pltpu.make_async_copy(cotangent, buf.mixed_one, field_sem.at[1])
    cotangent_again = pltpu.make_async_copy(cotangent, buf.y_shift, field_sem.at[2])
    output_store = pltpu.make_async_copy(buf.outgoing, out_ref, field_sem.at[3])
    grad_store = pltpu.make_async_copy(buf.outgoing, grad_ref, field_sem.at[4])
    token_load.start()
    cotangent_load.start()
    for copy in loads.values():
        copy.start()
    loads = SimpleNamespace(**loads)

    column = lax.broadcasted_iota(jnp.int32, (16, 128), 0)
    place = lax.broadcasted_iota(jnp.int32, (16, 128), 1) & 15
    chosen = jnp.where(column == ((place + 4) & 15), 1.0, 0.0).astype(BF)
    spread_region = dot_tn(region[...].astype(F32).astype(BF), chosen).reshape(8, 8, 128)
    row = lax.broadcasted_iota(jnp.int32, (8, 8, 128), 1)
    token = lax.broadcasted_iota(jnp.int32, (8, 8, 128), 2)
    own_row = jnp.where(row == (token >> 4), spread_region, 0.0)
    second = jnp.where(((token + 4) & 15) >= 8, 1.0, 0.0)[:, 0]
    buf.labels[...] = jnp.sum(own_row, axis=1) * 2.0 + second

    tokens_in = Halo(buf.window, halos[0], 1, 64)
    fine_back = Halo(buf.y_shift, halos[1], -1)
    grads_in = Halo(buf.normed_one, halos[2], 1)
    grads_back = Halo(buf.y_shift, halos[3], -1)
    skip_to_rows = Rows(buf.grad_mixed_two, buf.grad_skip_rows, row_sems[0])
    coarse_to_rows = Rows(buf.coarse, buf.coarse_rows, row_sems[1])
    level_to_tile = Rows(buf.level_two_rows, buf.level_two, row_sems[2])
    grad_to_tile = Rows(buf.grad_coarse_rows, buf.grad_coarse, row_sems[3])

    with jax.named_scope("tokens_in"):
        token_load.wait()
        tokens_in.pack(0)
        tokens_in.pack(1)
        pl.semaphore_wait(barrier, len(partners))
        tokens_in.start(range(4))

    with jax.named_scope("grad_skip"):
        cotangent_load.wait()

        def spread(at):
            spread_lanes(buf.spare, at, buf.mixed_one[block(at, 64)].astype(F32))

        loop(16, spread)

        def group_cotangent(at):
            buf.grouped[block(at, 16)] = jnp.concatenate(
                fine_pieces(buf.spare, at), axis=1
            ).astype(BF)

        loop(16, group_cotangent)

    def lanes(third, pair):
        return slice(C1 * third + 128 * pair, C1 * third + 128 * pair + 128)

    def windows_allowed(group):
        row = jnp.broadcast_to(buf.labels[pl.ds(group, 1), :], (128, 128))
        return row == row.T

    with jax.named_scope("level_one"):
        def write_window(at, rows):
            buf.window[block(at, 64)] = rows.astype(BF)
            buf.normed_one[block(at, 64)] = normalised(rows)[0].astype(BF)

        loads.qkv_one.wait()
        loads.proj_one.wait()
        for half in range(2):
            tokens_in.wait((3,) if half else (0, 1, 2))
            tokens_in.assemble(half, write_window)
            rows = slice(512 * half, 512 * half + 512)

            def project(at):
                buf.packed_one[rows, block(at, 256)] = dot(
                    buf.normed_one[rows], weight.qkv_one[:, block(at, 256)]
                ).astype(BF)

            loop(6, project, DENSE)

            def attend_group(at):
                group = at + 4 * half
                where = block(group, 128)
                units = [
                    [buf.packed_one[where, lanes(third, pair)] for third in range(3)]
                    for pair in range(4)
                ]
                for pair, found in enumerate(attend(units, windows_allowed(group))):
                    at_unit = group * 4 + pair
                    buf.expo_one[at_unit], buf.over_one[at_unit], mixed = found
                    buf.mixed_one[where, lanes(0, pair)] = mixed

            loop(4, attend_group, HEADS)

            def add_tokens(at):
                columns = block(at, 256)
                buf.y_shift[rows, columns] = (
                    buf.window[rows, columns].astype(F32)
                    + dot(buf.mixed_one[rows], weight.proj_one[:, columns])
                ).astype(BF)

            loop(2, add_tokens, DENSE)
            fine_back.pack(half)
            fine_back.start((0, 1, 2) if half == 0 else (3,))

    with jax.named_scope("merge"):
        loads.unmerge.wait()

        def grad_skip(at):
            buf.grad_mixed_two[:, block(at, 256)] = dot_nt(
                buf.grouped[...], weight.unmerge[block(at, 256)]
            ).astype(BF)

        loop(4, grad_skip, DENSE)
        skip_to_rows.start(0)
        skip_to_rows.start(1)

        def write_fine(at, rows):
            spread_lanes(buf.spare, at, rows.astype(BF).astype(F32))

        def group_fine(at):
            whole = jnp.concatenate(fine_pieces(buf.spare, at), axis=1)
            buf.fine[block(at, 16)] = whole.astype(BF)
            buf.grouped[block(at, 16)] = normalised(whole)[0].astype(BF)

        fine_back.wait((0, 1, 2))
        fine_back.assemble(0, write_fine)
        loop(8, lambda at: group_fine((at + 15) % 16))
        fine_back.wait((3,))
        fine_back.assemble(1, write_fine)
        loop(8, lambda at: group_fine(at + 7))
        loads.merge.wait()

        for half in range(2):
            rows = slice(128 * half, 128 * half + 128)

            def merge(at):
                columns = block(at, 256)
                buf.coarse[rows, columns] = dot(
                    buf.grouped[rows], weight.merge[:, columns]
                ).astype(BF)

            loop(4, merge, DENSE)
            coarse_to_rows.start(half)
        fine_back.drain()
        cotangent_again.start()

    with jax.named_scope("level_two"):
        loads.qkv_two.wait()
        loads.proj_two.wait()
        coarse_to_rows.wait()

        def norm_two(at):
            both = by_row(buf.coarse_rows[block(at, 64)].astype(F32), C2)
            for row in range(2):
                x = both[row].reshape(32, C2)
                where = pl.ds(pl.multiple_of(at * 32 + 128 * row, 32), 32)
                buf.wide[where] = x
                buf.normed_two[where] = normalised(x)[0].astype(BF)

        loop(4, norm_two)

        def project_two(at):
            columns = block(at, 256)
            buf.packed_two[:, columns] = dot(
                buf.normed_two[...], weight.qkv_two[:, columns]
            ).astype(BF)

        loop(12, project_two, DENSE)

        def operands_two(row, pair):
            rows = slice(128 * row, 128 * row + 128)
            return [
                buf.packed_two[rows, pl.ds(pl.multiple_of(C2 * third + pair * 128, 128), 128)]
                for third in range(3)
            ]

        def attend_two(at):
            places = [(2 * at + k, row) for k in range(2) for row in range(2)]
            units = [operands_two(row, pair) for pair, row in places]
            for (pair, row), found in zip(places, attend(units, None)):
                at_unit = pair * 2 + row
                buf.expo_two[at_unit], buf.over_two[at_unit], mixed = found
                buf.mixed_two[128 * row : 128 * row + 128, block(pair, 128)] = mixed

        loop(4, attend_two, HEADS)

        def add_coarse(at):
            columns = block(at, 256)
            total = buf.wide[:, columns] + dot(buf.mixed_two[...], weight.proj_two[:, columns])
            buf.level_two_rows[:, columns] = (
                jnp.stack([total[:128].reshape(16, 8, 256), total[128:].reshape(16, 8, 256)], axis=1)
                .reshape(256, 256)
                .astype(BF)
            )

        loop(4, add_coarse, DENSE)
        level_to_tile.start(0)
        level_to_tile.start(1)

    pair_copies = [
        remote(source, target, pair_send.at[k], pair_recv.at[k], device_of(moved(c, "core", 1)))
        for k, (source, target) in enumerate(
            (
                (buf.right_q.at[0:256], buf.right_q.at[256:512]),
                (buf.right_p.at[0:256], buf.right_p.at[256:512]),
                (buf.leave.at[0], buf.left_q.at[:, 256:512]),
                (buf.leave.at[1], buf.left_p.at[:, 256:512]),
            )
        )
    ]

    with jax.named_scope("grad_level_two"):
        skip_to_rows.wait()

        def grad_level(at):
            x = buf.level_two_rows[block(at, 64)].astype(F32)
            g = buf.grad_skip_rows[block(at, 64)].astype(F32)
            both = by_row(norm_back(x, g), C2)
            for row in range(2):
                where = pl.ds(pl.multiple_of(at * 32 + 128 * row, 32), 32)
                buf.right_p[where] = both[row].reshape(32, C2).astype(BF)

        loop(4, grad_level)
        pair_copies[1].start()
        skip_to_rows.drain()

        def grad_mixed(at):
            buf.grad_mixed_two[:, block(at, 256)] = dot_nt(
                buf.right_p[0:256], weight.proj_two[block(at, 256)]
            ).astype(BF)

        loop(4, grad_mixed, DENSE)

        def attend_two_back(at):
            places = [(2 * at + k, row) for k in range(2) for row in range(2)]
            units = []
            for pair, row in places:
                rows = slice(128 * row, 128 * row + 128)
                units.append(
                    operands_two(row, pair)
                    + [
                        buf.expo_two[pair * 2 + row],
                        buf.over_two[pair * 2 + row],
                        buf.mixed_two[rows, block(pair, 128)],
                        buf.grad_mixed_two[rows, block(pair, 128)],
                    ]
                )
            for (pair, row), found in zip(places, attend_back(units)):
                for third in range(3):
                    where = pl.ds(pl.multiple_of(C2 * third + pair * 128, 128), 128)
                    buf.right_q[128 * row : 128 * row + 128, where] = found[third]

        loop(4, attend_two_back, HEADS)

    def turn(source, left, slot):
        first = c["core"] == 0
        for half in range(2):
            tokens_at = slice(128 * half, 128 * half + 128)
            groups = source[tokens_at].astype(F32).T.reshape(64, 2, 8, 128)
            mine = jnp.where(first, groups[:, 0], groups[:, 1])
            theirs = jnp.where(first, groups[:, 1], groups[:, 0])
            left[:, tokens_at] = mine.reshape(512, 128).astype(BF)
            buf.leave[slot, :, tokens_at] = theirs.reshape(512, 128).astype(BF)

    with jax.named_scope("grad_coarse"):
        pair_copies[0].start()

        def grad_normed_two(at):
            buf.grad_mixed_two[:, block(at, 256)] = dot_nt(
                buf.right_q[0:256], weight.qkv_two[block(at, 256)]
            ).astype(BF)

        loop(4, grad_normed_two, DENSE)

        def grad_coarse(at):
            both = []
            for row in range(2):
                where = pl.ds(pl.multiple_of(at * 32 + 128 * row, 32), 32)
                g = norm_back(buf.wide[where], buf.grad_mixed_two[where].astype(F32))
                g = g.astype(BF).astype(F32) + buf.right_p[where].astype(F32)
                both.append(g.reshape(4, 8, C2))
            buf.grad_coarse_rows[block(at, 64)] = (
                jnp.stack(both, axis=1).reshape(64, C2).astype(BF)
            )

        for half in range(2):
            loop(2, lambda at: grad_coarse(at + 2 * half))
            grad_to_tile.start(half)

    with jax.named_scope("weight_gradients"):
        turn(buf.normed_two, buf.left_q, 0)
        pair_copies[2].start()
        turn(buf.mixed_two, buf.left_p, 1)
        pair_copies[3].start()
        for copy in pair_copies:
            copy.wait_recv()

        def put_total(zh, columns, top, low):
            width = top.shape[1]
            both = jnp.concatenate([top.reshape(32, 8, width), low.reshape(32, 8, width)], axis=1)
            reducer.total[zh, :, :, :, :, columns] = both.astype(BF).reshape(4, 2, 4, 16, width)

        def narrow_tile(at):
            right = jnp.concatenate(
                [buf.right_q[:, block(at, 128)], buf.right_q[:, block(at + 16, 128)]], axis=1
            )
            for zh in range(2):
                both = dot(buf.left_q[256 * zh : 256 * zh + 256], right)
                put_total(zh, block(at, 128), both[:, :128], both[:, 128:])

        def wide_tile(at):
            for zh in range(2):
                rows = slice(256 * zh, 256 * zh + 256)
                top = dot(buf.left_q[rows], buf.right_q[:, block(at, 256)])
                low = dot(buf.left_p[rows], buf.right_p[:, block(at - 4, 256)])
                put_total(zh, block(at, 256), top, low)

        for part, (start, stop, _) in enumerate(PARTS):
            middle = max(start, min(stop, 1024))
            if middle > start:
                loop((middle - start) // 128, lambda at: narrow_tile(at + start // 128), TILES)
            if stop > middle:
                loop((stop - middle) // 256, lambda at: wide_tile(at + middle // 256), TILES)
            reducer.start(part, 0)

    with jax.named_scope("grad_fine"):
        grad_to_tile.wait()

        def grad_grouped(at):
            buf.grouped[:, block(at, 256)] = dot_nt(
                buf.grad_coarse[...], weight.merge[block(at, 256)]
            ).astype(BF)

        loop(8, grad_grouped, DENSE)
        for part in range(3):
            reducer.pass_on(part)

        def grad_pieces(at):
            g = norm_back(
                buf.fine[block(at, 16)].astype(F32), buf.grouped[block(at, 16)].astype(F32)
            )
            put_pieces(buf.spare, at, [g[:, C1 * k : C1 * k + C1] for k in range(4)])

        loop(16, grad_pieces)

        cotangent_again.wait()

        def grad_fine(at):
            buf.normed_one[block(at, 64)] = (
                joined_rows(buf.spare, at, C1) + buf.y_shift[block(at, 64)].astype(F32)
            ).astype(BF)

        loop(16, grad_fine)
        grads_in.pack(0)
        grads_in.pack(1)
        grads_in.start(range(4))

    with jax.named_scope("output"):
        level_to_tile.wait()

        def norm_level(at):
            x = buf.level_two[block(at, 64)].astype(F32)
            buf.coarse[block(at, 64)] = normalised(x)[0].astype(BF)

        coarse_to_rows.drain()
        loop(4, norm_level)

        for half in range(2):
            rows = slice(128 * half, 128 * half + 128)

            def unmerge(at):
                for low in range(2):
                    buf.wide[128 * low : 128 * low + 128, block(at, 256)] = dot(
                        buf.coarse[rows], weight.unmerge[:, block(at + 4 * low, 256)]
                    )

            loop(4, unmerge, DENSE)

            def add_fine(at):
                fine = buf.fine[block(at + 8 * half, 16)].astype(F32)
                upper = jnp.concatenate(
                    [buf.wide[block(at, 16)], buf.wide[block(at + 8, 16)]], axis=1
                )
                total = fine + upper
                put_pieces(
                    buf.spare,
                    at + 8 * half,
                    [total[:, C1 * k : C1 * k + C1] for k in range(4)],
                )

            loop(8, add_fine)

        def write_output(at):
            buf.outgoing[block(at, 64)] = joined_rows(buf.spare, at, C1).astype(BF)

        loop(16, write_output)
        output_store.start()

    with jax.named_scope("grad_level_one"):

        def write_grads(at, rows):
            buf.y_shift[block(at, 64)] = rows.astype(BF)

        for half in range(2):
            grads_in.wait((3,) if half else (0, 1, 2))
            grads_in.assemble(half, write_grads)
            if half:
                grads_in.drain()
            rows = slice(512 * half, 512 * half + 512)

            def grad_mixed_one(at):
                buf.normed_one[rows, block(at, 256)] = dot_nt(
                    buf.y_shift[rows], weight.proj_one[block(at, 256)]
                ).astype(BF)

            loop(2, grad_mixed_one, DENSE)

            def attend_group_back(at):
                group = at + 4 * half
                where = block(group, 128)
                units = []
                for pair in range(4):
                    at_unit = group * 4 + pair
                    units.append(
                        [buf.packed_one[where, lanes(third, pair)] for third in range(3)]
                        + [
                            buf.expo_one[at_unit],
                            buf.over_one[at_unit],
                            buf.mixed_one[where, lanes(0, pair)],
                            buf.normed_one[where, lanes(0, pair)],
                        ]
                    )
                for pair, found in enumerate(attend_back(units)):
                    for third in range(3):
                        buf.packed_one[where, lanes(third, pair)] = found[third]

            loop(4, attend_group_back, HEADS)
            for part in range(3):
                reducer.finish(part, half)
                reducer.start(part, half + 1)

            def grad_normed_one(at):
                buf.normed_one[rows, block(at, 256)] = dot_nt(
                    buf.packed_one[rows], weight.qkv_one[block(at, 256)]
                ).astype(BF)

            loop(2, grad_normed_one, DENSE)

            def grad_window(at):
                where = block(at + 8 * half, 64)
                g = norm_back(
                    buf.window[where].astype(F32), buf.normed_one[where].astype(F32)
                )
                buf.y_shift[where] = (g + buf.y_shift[where].astype(F32)).astype(BF)

            loop(8, grad_window)
            grads_back.pack(half)
            grads_back.start((0, 1, 2) if half == 0 else (3,))

    with jax.named_scope("grad_tokens"):
        output_store.wait()

        def write_tokens(at, rows):
            buf.outgoing[block(at, 64)] = rows.astype(BF)

        grads_back.wait((0, 1, 2))
        grads_back.assemble(0, write_tokens)
        grads_back.wait((3,))
        grads_back.assemble(1, write_tokens)
        grad_store.start()
        for part in range(3):
            store_folded(part, reducer.finish(part, 2), qkv_ref, proj_ref)

    tokens_in.drain()
    grads_back.drain()
    level_to_tile.drain()
    grad_to_tile.drain()
    for copy in pair_copies:
        copy.wait_send()
    reducer.drain()
    grad_store.wait()


def hand_over(*refs):
    for source, target in zip(refs[:4], refs[4:]):
        target[...] = source[...]


def body(
    tokens, region, qkv_one, proj_one, merge_weight, qkv_two, proj_two, unmerge_weight, cotangent
):
    vmem = pl.BlockSpec(memory_space=pltpu.VMEM)
    anywhere = pl.BlockSpec(memory_space=pl.ANY)
    shapes = (
            jax.ShapeDtypeStruct((TOKENS, C1), BF),
            jax.ShapeDtypeStruct((TOKENS, C1), BF),
            jax.ShapeDtypeStruct((8, 3 * C2), F32),
            jax.ShapeDtypeStruct((8, C2), F32),
    )
    found = pl.pallas_call(
        whole_kernel,
        out_shape=shapes,
        in_specs=[vmem] + [anywhere] * 8,
        out_specs=(anywhere, anywhere, vmem, vmem),
        scratch_shapes=scratch_list(),
        compiler_params=pltpu.CompilerParams(
            collective_id=0, has_side_effects=True, vmem_limit_bytes=VMEM_LIMIT
        ),
    )(
        region.T,
        tokens.reshape(TOKENS, C1),
        cotangent.reshape(TOKENS, C1),
        unmerge_weight,
        qkv_one,
        proj_one,
        merge_weight,
        qkv_two,
        proj_two,
    )
    pieces = [
        pl.BlockSpec((TOKENS // 2, C1), lambda at: (at, 0)),
        pl.BlockSpec((TOKENS // 2, C1), lambda at: (at, 0)),
        pl.BlockSpec((8, 3 * C2 // 2), lambda at: (0, at)),
        pl.BlockSpec((8, C2 // 2), lambda at: (0, at)),
    ]
    output, grad_tokens, grad_qkv_two, grad_proj_two = pl.pallas_call(
        hand_over, grid=(2,), out_shape=shapes, in_specs=pieces, out_specs=pieces
    )(*found)
    shape = tokens.shape
    return output.reshape(shape), grad_tokens.reshape(shape), grad_qkv_two, grad_proj_two


def solution(mesh):
    return jax.shard_map(
        body,
        mesh=mesh,
        in_specs=(
            P("lat", "lon", None),
            P("lat", "lon"),
            P(),
            P(),
            P(),
            P(),
            P(),
            P(),
            P("lat", "lon", None),
        ),
        out_specs=(
            P("lat", "lon", None),
            P("lat", "lon", None),
            P(("lat", "lon"), None),
            P(("lat", "lon"), None),
        ),
        check_vma=False,
    )
```
